512 devices in a mesh: ctx: 64 (over y, z), kvh: 8 (over x, core).
Axes of the slice: x: 4, y: 8, z: 8, core: 2. Of those that a mesh axis runs over, the one named last changes fastest.
Arguments:
- queries: bfloat16 [8192, 8192], P(('ctx', 'kvh')), may hold values from -8 to 8
- keys: bfloat16 [8, 131072, 128], P('kvh', 'ctx'), may hold values from -4 to 4
- values: bfloat16 [8, 131072, 128], P('kvh', 'ctx'), may hold values from -6 to 6
- vertical: int32 [8, 8], P('kvh'), may hold values from 0 to 2047, as said below
- slash_blocks: int32 [8, 128, 32], P('kvh', 'ctx'), may hold values from 0 to 2047, as said below
- slash_count: int32 [8, 128], P('kvh', 'ctx'), may hold values from 4 to 32
- row_order: int32 [8, 128], P('kvh', 'ctx'), may hold values from 0 to 127, as said below
Outputs:
- attended: bfloat16 [8192, 8192], P(('ctx', 'kvh'))
The draws below stay inside these ranges and needn't reach their ends.
Inputs may be any that keep to these rules, and one draw needn't show every extreme that they name: Key block k lies on ctx device k // 32; the 8 vertical blocks of a KV head lie on 8 different ctx devices. `slash_blocks`: only the first slash_count entries of a query block are used; they are distinct and none is a vertical block of the same KV head. Taking the used entries of all query blocks of a ctx device and of its partner (the device whose ctx index differs by half of the ctx axis) together, at most 2 distinct key blocks lie on any one ctx device, and this bound is reached in every draw. `row_order`: each KV head's row is a permutation of the query blocks. Output slot s lies on ctx device s // 2; of a device's 2 slots, the first 1 name query blocks of that device in increasing order, the last 1 name query blocks of its partner in increasing order.
All inputs are finite; a program needn't handle non-finite values.
Results may differ from the reference program's by a relative error of at most 0.0047.
Values may be sent and summed in bfloat16 or wider, within the bound.
A program may use at most 64 MiB of HBM per device.

```python
import math
import jax
import jax.numpy as jnp
from jax import lax

HD = 128
QH = 8
KV_HEADS = 8
BLK = 64
VERT = 8
SMAX = 32
CAP = 2
QB_DEV = 2
KB_DEV = 32
MOVE = 1
QB = 128
KB = 2048
QTOK = 8192
KEYS = 131072


def head_pattern(key):
    ndev = QB // QB_DEV
    half = ndev // 2
    subkeys = jax.random.split(key, 5)
    owners = jax.random.permutation(subkeys[0], ndev)
    column_local = jax.random.randint(subkeys[1], (ndev,), 0, KB_DEV)
    column_owner = owners[:VERT]
    columns = column_owner * KB_DEV + column_local[column_owner]

    def pair_pool(pair_key):
        first_key, second_key = jax.random.split(pair_key)
        owner_order = jax.random.permutation(first_key, ndev)
        picks = jax.vmap(lambda inner: jax.random.permutation(inner, KB_DEV - 1)[:CAP])(jax.random.split(second_key, ndev))
        local = (column_local[:, None] + 1 + picks) % KB_DEV
        block_ids = jnp.arange(ndev)[:, None] * KB_DEV + local
        return block_ids[owner_order].reshape(-1)
    pools = jax.vmap(pair_pool)(jax.random.split(subkeys[2], half))
    lower_heavy = jax.random.randint(subkeys[3], (half,), 0, 2)
    device = jnp.arange(ndev)
    upper = device // half
    heavy = jnp.where(upper == 1, 1 - lower_heavy[device % half], lower_heavy[device % half])
    lowest = jnp.where(heavy == 1, SMAX * 5 // 8, SMAX // 8)
    spread = jnp.where(heavy == 1, SMAX - SMAX * 5 // 8 + 1, 3 * SMAX // 8 - SMAX // 8 + 1)
    raw = jax.random.randint(subkeys[4], (ndev, QB_DEV), 0, 1 << 20)
    counts = lowest[:, None] + raw % spread[:, None]
    counts = counts.at[:, 0].set(jnp.where(heavy == 1, SMAX, counts[:, 0]))
    pair_counts = jnp.concatenate([counts[:half], counts[half:]], axis=1)
    used = jnp.arange(SMAX)[None, None, :] < pair_counts[:, :, None]
    flat = used.reshape(half, -1).astype(jnp.int32)
    ranked = jnp.cumsum(flat, axis=1) - 1
    position = jnp.where(flat == 1, ranked, jnp.arange(flat.shape[1])[None, :]) % (ndev * CAP)
    chosen = jnp.take_along_axis(pools, position, axis=1).reshape(half, 2, QB_DEV, SMAX)
    lists = chosen.transpose(1, 0, 2, 3).reshape(QB, SMAX)
    index_row = jnp.arange(QB_DEV)
    score = jnp.where(heavy[:, None] == 1, counts, SMAX - counts) * QB_DEV + (QB_DEV - 1 - index_row)[None, :]
    unused_values, sent = lax.top_k(score, MOVE)
    sent_mask = jnp.any(index_row[None, :, None] == sent[:, None, :], axis=2).astype(jnp.int32)
    stay_order = jnp.argsort(sent_mask * QB_DEV + index_row[None, :], axis=1)[:, :QB_DEV - MOVE]
    sent_order = jnp.argsort((1 - sent_mask) * QB_DEV + index_row[None, :], axis=1)[:, :MOVE]
    partner = (device + half) % ndev
    order = jnp.concatenate([device[:, None] * QB_DEV + stay_order, partner[:, None] * QB_DEV + sent_order[partner]], axis=1)
    return (columns.astype(jnp.int32), lists.astype(jnp.int32), counts.reshape(QB).astype(jnp.int32), order.reshape(QB).astype(jnp.int32))


def pattern(key):
    return jax.vmap(head_pattern)(jax.random.split(key, KV_HEADS))


def draw_vertical(key, part):
    shared = pattern(key)
    return shared[0]


def draw_slash_blocks(key, part):
    shared = pattern(key)
    return shared[1]


def draw_slash_count(key, part):
    shared = pattern(key)
    return shared[2]


def draw_row_order(key, part):
    shared = pattern(key)
    return shared[3]


def draw_queries(key, part):
    key = jax.random.fold_in(key, 15)
    base = jax.random.truncated_normal(key, -4.0, 4.0, (QTOK, KV_HEADS * QH * HD), jnp.float32)
    return base.astype(jnp.bfloat16)


def draw_keys(key, part):
    key = jax.random.fold_in(key, 16)
    base = jax.random.truncated_normal(key, -4.0, 4.0, (KV_HEADS, KEYS, HD), jnp.float32)
    return base.astype(jnp.bfloat16)


def shard_levels(rng, dims, cuts, smallest, high):
    level = 1.0
    for dim, blocks in cuts:
        heights = jax.random.uniform(jax.random.fold_in(jax.random.fold_in(rng, 6), dim), (blocks,), jnp.float32, smallest / len(cuts), high / len(cuts))
        level = level * jnp.repeat(jnp.exp(heights), dims[dim] // blocks).reshape((-1,) + (1,) * (len(dims) - 1 - dim))
    return level


def scatter_about(own_key, extent, deviation, reach, pieces=(), dtype=jnp.bfloat16):
    factor_of = shard_levels(own_key, extent, pieces, -0.22, 0.18) if pieces else 1.0
    drawn = jax.random.normal(own_key, extent, jnp.float32) * deviation * factor_of
    return jnp.minimum(jnp.maximum(drawn, -reach), reach).astype(dtype)


def setup_inputs(seed: int = 0) -> dict:
    key_of = jax.random.split(jax.random.key(seed), 8)
    queries = draw_queries(jax.random.fold_in(key_of[7], 71), 0)
    keys = draw_keys(jax.random.fold_in(key_of[7], 71), 0)
    values = scatter_about(key_of[2], (KV_HEADS, KEYS, HD), 1.0, 6.0, ((0, 8), (1, 64)))
    vertical = draw_vertical(jax.random.fold_in(key_of[7], 71), 0)
    slash_blocks = draw_slash_blocks(jax.random.fold_in(key_of[7], 71), 0)
    slash_count = draw_slash_count(jax.random.fold_in(key_of[7], 71), 0)
    row_order = draw_row_order(jax.random.fold_in(key_of[7], 71), 0)
    return dict(queries=queries, keys=keys, values=values, vertical=vertical, slash_blocks=slash_blocks, slash_count=slash_count, row_order=row_order)


def attend_head(q_head, k_head, v_head, columns, lists, counts, order):
    key_blocks = k_head.reshape(KB, BLK, HD)
    value_blocks = v_head.reshape(KB, BLK, HD)
    scale = 1.0 / math.sqrt(HD)

    def one_block(item):
        query_block, row_list, count = item
        picked = jnp.concatenate([columns, row_list]).astype(jnp.int32)
        key_rows = key_blocks[picked].reshape(-1, HD).astype(jnp.float32)
        value_rows = value_blocks[picked].reshape(-1, HD).astype(jnp.float32)
        alive = jnp.concatenate([jnp.ones((VERT,), bool), jnp.arange(SMAX) < count])
        alive = jnp.repeat(alive, BLK)
        scores = jnp.einsum('tgd,kd->tgk', query_block.astype(jnp.float32), key_rows) * scale
        scores = jnp.where(alive, scores, -jnp.inf)
        peak = lax.optimization_barrier(jnp.max(scores, axis=-1, keepdims=True))
        weights = jnp.exp(scores - peak)
        total = lax.optimization_barrier(jnp.sum(weights, axis=-1))
        rounded = weights.astype(jnp.bfloat16).astype(jnp.float32)
        mixed = jnp.einsum('tgk,kd->tgd', rounded, value_rows)
        return (mixed / total[..., None]).astype(jnp.bfloat16)
    results = lax.map(one_block, (q_head, lists, counts))
    return results[order]

def reference(queries, keys, values, vertical, slash_blocks, slash_count, row_order):
    per_head = queries.reshape(QB, BLK, KV_HEADS, QH, HD).transpose(2, 0, 1, 3, 4)
    results = lax.map(lambda item: attend_head(*item), (per_head, keys, values, vertical, slash_blocks, slash_count, row_order))
    return results.transpose(1, 2, 0, 3, 4).reshape(QB * BLK, KV_HEADS * QH * HD)
```

```python
import math

import jax
import jax.numpy as jnp
from jax import lax
from jax.experimental import pallas as pl
from jax.experimental.pallas import tpu as pltpu
from jax.sharding import PartitionSpec as P

MESH = pl.DeviceIdType.MESH
BLK = 64
HD = 128
QH = 8
NY = 8
NZ = 8
NCTX = NY * NZ
NKV = 8
WIDTH = QH * HD
TOK = 16
SMAX = 32
STAT = WIDTH + 128
NEG = -1e30
SCALE2 = math.log2(math.e) / math.sqrt(HD)
LOG2E = math.log2(math.e)
ROUTES = ((0, 0, 2, (0, 1)), (-1, 2, 2, (0, 1)), (1, 4, 2, (0, 1)), (-2, 6, 1, (0,)), (2, 7, 1, (1,)))
SEND_ORDER = (4, 3, 5, 2, 6, 1, 7, 0)
WORK_ORDER = (0, 4, 3, 5, 2, 6, 1, 7)


def wait_for(ref, sem):
    pltpu.make_async_copy(ref, ref, sem).wait()


def kernel(
    q_ref, k_ref, v_ref, vert_ref, lists_ref, cnt_ref, ord_ref, out_ref,
    kbuf, vbuf, mrow, mall, msm, pickv, picks, qbuf, q2, stag, kv, va, vb, vc,
    acc, mx, ls, bias, ostage, orecv,
    lsem, s_meta, s_q, s_va, s_vb, s_vc, s_kv, s_out,
    r_meta, r_q, r_va, r_vb, r_vc, r_kv, r_out,
):
    me = lax.axis_index("ctx")
    h = lax.axis_index("kvh")
    y, z = me // NZ, me % NZ

    def at(yy, zz):
        return lax.rem(yy + 2 * NY, NY) * NZ + lax.rem(zz + 2 * NZ, NZ)

    def push(src, dst, ssem, rsem, ctx, kvh):
        pltpu.make_async_remote_copy(
            src_ref=src, dst_ref=dst, send_sem=ssem, recv_sem=rsem,
            device_id=(ctx, kvh), device_id_type=MESH,
        ).start()

    load_k = pltpu.make_async_copy(k_ref, kbuf, lsem.at[0])
    load_v = pltpu.make_async_copy(v_ref, vbuf, lsem.at[1])
    load_k.start()
    load_v.start()

    homes = (at(y + 2, z), at(y - 2, z))

    barrier = pltpu.get_barrier_semaphore()

    def greet(t, _):
        pl.semaphore_signal(
            barrier, inc=1, device_id=(lax.rem(me + t, NCTX), h), device_id_type=MESH
        )
        return 0

    lax.fori_loop(1, NCTX, greet, 0)
    for home in homes:
        def greet_heads(t, _, home=home):
            pl.semaphore_signal(
                barrier, inc=1, device_id=(home, lax.rem(h + t, NKV)), device_id_type=MESH
            )
            return 0

        lax.fori_loop(1, NKV, greet_heads, 0)

    lane = lax.broadcasted_iota(jnp.int32, (1, 128), 1)
    mrow[0] = jnp.full((1, 128), -1, jnp.int32)
    mrow[0, :, 0:SMAX] = lists_ref[0, 0:1, :]
    mrow[0, :, SMAX:2 * SMAX] = lists_ref[0, 1:2, :]
    row = mrow[0]
    limit = jnp.where(lane < SMAX, cnt_ref[0, 0], cnt_ref[0, 1] + SMAX)
    row = jnp.where(lane < limit, row, -1)
    row = jnp.where(lane == 2 * SMAX, ord_ref[0, 0], row)
    row = jnp.where(lane == 2 * SMAX + 1, ord_ref[0, 1], row)
    mrow[0] = row
    mall[me] = row

    pl.semaphore_wait(barrier, NCTX - 1 + 2 * (NKV - 1))

    def send_meta(t, _):
        push(mrow.at[0], mall.at[me], s_meta, r_meta, lax.rem(me + t, NCTX), h)
        return 0

    lax.fori_loop(1, NCTX, send_meta, 0)

    token_rows = pl.ds(pl.multiple_of(lax.rem(h, 4) * TOK, TOK), TOK)
    for where in range(2):
        target = homes[1 - where]
        for t in range(NKV):
            push(
                q_ref.at[:, pl.ds(t * WIDTH, WIDTH)],
                qbuf.at[where * 2 + h // 4, token_rows, :],
                s_q, r_q, target, t,
            )

    load_k.wait()
    load_v.wait()
    mine = jnp.int32(0)
    for i in range(NKV):
        entry = vert_ref[0, i]
        mine = jnp.where(entry // 32 == me, lax.rem(entry, 32), mine)
    va[0, 0] = kbuf[mine]
    va[0, 1] = vbuf[mine]
    for a in range(1, NY):
        push(va.at[0], va.at[a], s_va, r_va, at(y + a, z), h)

    wait_for(mall.at[pl.ds(0, NCTX - 1)], r_meta)
    low = mall[0:NCTX // 2].reshape(NCTX // 2, 128)
    high = mall[NCTX // 2:NCTX].reshape(NCTX // 2, 128)
    wide = lax.broadcasted_iota(jnp.int32, (NCTX // 2, 128), 1)
    entries = jnp.where(wide < 2 * SMAX, low, pltpu.roll(high, 2 * SMAX, 1))
    own = lax.shift_right_arithmetic(entries, 5) == me
    local = entries & 31
    first = jnp.min(jnp.where(own, local, 99), axis=1, keepdims=True)
    last = jnp.max(jnp.where(own, local, 0), axis=1, keepdims=True)
    first = jnp.where(first == 99, 0, first)
    pickv[...] = jnp.where(wide == 0, first, last)
    to_picks = pltpu.make_async_copy(pickv, picks, lsem.at[2])
    to_picks.start()
    to_msm = [
        pltpu.make_async_copy(mall.at[homes[i]], msm.at[i], lsem.at[3 + i]) for i in range(2)
    ]
    for copy in to_msm:
        copy.start()
    to_picks.wait()

    for dz in SEND_ORDER:
        for dy, start, count, which in ROUTES:
            pair = lax.rem(y + dy + 2 + NY, 4) * NZ + lax.rem(z + dz, NZ)
            here = dz == 0 and dy == 0
            for i in range(count):
                pick = picks[pair, which[i]]
                if here:
                    kv[dz, start + i, 0] = kbuf[pick]
                    kv[dz, start + i, 1] = vbuf[pick]
                else:
                    stag[dz, start + i, 0] = kbuf[pick]
                    stag[dz, start + i, 1] = vbuf[pick]
            if not here:
                span = pl.ds(start, count)
                push(
                    stag.at[dz, span], kv.at[dz, span], s_kv.at[dz], r_kv.at[dz],
                    at(y + dy, z + dz), h,
                )

    owner = vert_ref[0, y] // 32
    near = lax.rem(y - owner // NZ + NY, NY)
    wait_for(va.at[pl.ds(1, NY - 1)], r_va)
    vb[0] = va[near]
    for b in range(1, NZ):
        push(vb.at[0], vb.at[b], s_vb, r_vb, at(y, z + b), h)

    for copy in to_msm:
        copy.wait()
    slot = lax.broadcasted_iota(jnp.int32, (NZ, 8 * BLK), 1) // BLK
    back = lax.broadcasted_iota(jnp.int32, (NZ, 8 * BLK), 0)
    step = jnp.where(slot < 2, 0, jnp.where(slot < 4, 1, jnp.where(slot < 6, -1, jnp.where(slot == 6, 2, -2))))
    source = ((y + step) & (NY - 1)) * NZ + ((z - back) & (NZ - 1))

    def scan(t, carry):
        lo, hi = carry
        for i in range(2):
            entry = msm[i, 0, t]
            hit = source == lax.shift_right_arithmetic(entry, 5)
            lo = jnp.where(hit, jnp.minimum(lo, entry), lo)
            hi = jnp.where(hit, jnp.maximum(hi, entry), hi)
        return lo, hi

    lo, hi = lax.fori_loop(
        0, 2 * SMAX, scan,
        (jnp.full((NZ, 8 * BLK), 1 << 20, jnp.int32), jnp.full((NZ, 8 * BLK), -3, jnp.int32)),
    )
    second = (slot == 1) | (slot == 3) | (slot == 5) | (slot == 7)
    held = jnp.where(second, jnp.where(hi > lo, hi, -2), lo)

    stay = msm[0, 0, 2 * SMAX] & 1
    came = msm[0, 0, 2 * SMAX + 1] & 1
    source_block = (stay, 2 + came, 3 - came, 1 - stay)
    for r in range(4):
        block = source_block[r]
        side = block // 2
        first_entry = lax.rem(block, 2) * SMAX

        def member(t, need, side=side, first_entry=first_entry):
            return need | (held == msm[side, 0, first_entry + t]).astype(jnp.int32)

        need = lax.fori_loop(0, SMAX, member, jnp.zeros((NZ, 8 * BLK), jnp.int32))
        bias[r] = jnp.where(need > 0, 0.0, NEG)

    wait_for(qbuf, r_q)
    for r in range(4):
        for g in range(QH):
            q2[r * 2 + g // 4, pl.ds((g % 4) * BLK, BLK), :] = qbuf[
                source_block[r], :, pl.ds(g * HD, HD)
            ]
    for i in range(8):
        acc[i] = jnp.zeros((256, HD), jnp.float32)
        ls[i] = jnp.zeros((256, 128), jnp.float32)
        mx[i] = jnp.full((256, 128), NEG, jnp.float32)

    near = lax.rem(z - lax.rem(owner, NZ) + NZ, NZ)
    wait_for(vb.at[pl.ds(1, NZ - 1)], r_vb)
    index = lax.rem(y, 4)
    vc[index] = vb[near]
    for t in range(1, 4):
        push(
            vc.at[index], vc.at[index], s_vc, r_vc,
            at((y // 4) * 4 + lax.rem(index + t, 4), z), h,
        )

    def attend(load, size, dz):
        def body(i, _):
            keys, values = load()
            scores = lax.dot_general(
                q2[i], keys, (((1,), (1,)), ((), ())), preferred_element_type=jnp.float32
            )
            if dz is not None:
                scores = scores + bias[i // 2, dz:dz + 1, :]
            old = mx[i]
            new = jnp.maximum(old, jnp.max(scores, axis=1, keepdims=True))
            shrink = jnp.exp2((old - new) * SCALE2)
            peak = new * SCALE2
            weights = jnp.exp2(scores * SCALE2 - jnp.concatenate([peak] * (size // 128), axis=1))
            total = weights[:, 0:128]
            for j in range(1, size // 128):
                total = total + weights[:, j * 128:(j + 1) * 128]
            ls[i] = ls[i] * shrink + total
            acc[i] = acc[i] * shrink + jnp.dot(
                weights.astype(jnp.bfloat16), values, preferred_element_type=jnp.float32
            )
            mx[i] = new
            return 0

        lax.fori_loop(0, 8, body, 0)

    def chunk(dz):
        def load():
            return kv[dz, :, 0].reshape(8 * BLK, HD), kv[dz, :, 1].reshape(8 * BLK, HD)

        if dz == 0:
            wait_for(kv.at[0, pl.ds(2, 6)], r_kv.at[0])
        else:
            wait_for(kv.at[dz], r_kv.at[dz])
        attend(load, 8 * BLK, dz)

    chunk(WORK_ORDER[0])
    wait_for(vc.at[pl.ds(0, 3)], r_vc)
    attend(
        lambda: (vc[:, 0].reshape(4 * BLK, HD), vc[:, 1].reshape(4 * BLK, HD)), 4 * BLK, None
    )
    for dz in WORK_ORDER[1:]:
        chunk(dz)

    lanes = lax.broadcasted_iota(jnp.int32, (BLK, 128), 1)

    def finish(r, _):
        stats = jnp.zeros((BLK, 128), jnp.float32)
        for half in range(2):
            i = r * 2 + half
            total = jnp.sum(ls[i], axis=1, keepdims=True)
            mixed = acc[i] / total
            weight = mx[i] * SCALE2 + jnp.log(total) * LOG2E
            big = weight.astype(jnp.bfloat16).astype(jnp.float32)
            rest = weight - big
            mid = rest.astype(jnp.bfloat16).astype(jnp.float32)
            tail = rest - mid
            for j in range(4):
                g = half * 4 + j
                rows = slice(j * BLK, (j + 1) * BLK)
                ostage[r, :, g * HD:(g + 1) * HD] = mixed[rows].astype(jnp.bfloat16)
                stats = jnp.where(lanes == g, big[rows], stats)
                stats = jnp.where(lanes == QH + g, mid[rows], stats)
                stats = jnp.where(lanes == 2 * QH + g, tail[rows], stats)
        ostage[r, :, WIDTH:STAT] = stats.astype(jnp.bfloat16)
        return 0

    lax.fori_loop(0, 4, finish, 0)
    for i in range(2):
        for t in range(NKV):
            push(
                ostage.at[i * 2 + t // 4, pl.ds((t % 4) * TOK, TOK), :],
                orecv.at[i, h], s_out, r_out, homes[i], t,
            )

    wait_for(orecv, r_out)
    for head in range(NKV):
        logs = []
        for i in range(2):
            terms = orecv[i, head, :, WIDTH:STAT].astype(jnp.float32)
            logs.append(terms + pltpu.roll(terms, 128 - QH, 1) + pltpu.roll(terms, 128 - 2 * QH, 1))
        share = 1.0 / (1.0 + jnp.exp2(logs[1] - logs[0]))
        for g in range(QH):
            cols = slice(g * HD, (g + 1) * HD)
            part = share[:, g:g + 1]
            one = orecv[0, head, :, cols].astype(jnp.float32)
            two = orecv[1, head, :, cols].astype(jnp.float32)
            out_ref[:, head * WIDTH + g * HD:head * WIDTH + (g + 1) * HD] = (
                one * part + two * (1.0 - part)
            ).astype(jnp.bfloat16)

    wait_for(mall.at[pl.ds(0, NCTX - 1)], s_meta)
    wait_for(qbuf, s_q)
    wait_for(va.at[pl.ds(1, NY - 1)], s_va)
    wait_for(vb.at[pl.ds(1, NZ - 1)], s_vb)
    wait_for(vc.at[pl.ds(0, 3)], s_vc)
    wait_for(stag.at[0, pl.ds(2, 6)], s_kv.at[0])
    for dz in range(1, NZ):
        wait_for(stag.at[dz], s_kv.at[dz])
    wait_for(ostage, s_out)


def per_device(queries, keys, values, vertical, slash_blocks, slash_count, row_order):
    bf16, f32, i32 = jnp.bfloat16, jnp.float32, jnp.int32
    blocks = keys.shape[1] // BLK
    vmem = pltpu.VMEM
    dma = pltpu.SemaphoreType.DMA
    any_spec = pl.BlockSpec(memory_space=pl.ANY)
    vmem_spec = pl.BlockSpec(memory_space=pltpu.VMEM)
    smem_spec = pl.BlockSpec(memory_space=pltpu.SMEM)
    return pl.pallas_call(
        kernel,
        out_shape=jax.ShapeDtypeStruct(queries.shape, bf16),
        in_specs=[any_spec, any_spec, any_spec, smem_spec, vmem_spec, smem_spec, smem_spec],
        out_specs=vmem_spec,
        scratch_shapes=[
            vmem((blocks, BLK, HD), bf16),
            vmem((blocks, BLK, HD), bf16),
            vmem((1, 1, 128), i32),
            vmem((NCTX, 1, 128), i32),
            pltpu.SMEM((2, 1, 128), i32),
            vmem((NCTX // 2, 128), i32),
            pltpu.SMEM((NCTX // 2, 128), i32),
            vmem((4, BLK, WIDTH), bf16),
            vmem((8, 256, HD), bf16),
            vmem((NZ, 8, 2, BLK, HD), bf16),
            vmem((NZ, 8, 2, BLK, HD), bf16),
            vmem((NY, 2, BLK, HD), bf16),
            vmem((NZ, 2, BLK, HD), bf16),
            vmem((4, 2, BLK, HD), bf16),
            vmem((8, 256, HD), f32),
            vmem((8, 256, 128), f32),
            vmem((8, 256, 128), f32),
            vmem((4, NZ, 8 * BLK), f32),
            vmem((4, BLK, STAT), bf16),
            vmem((2, NKV, TOK, STAT), bf16),
            dma((5,)),
            dma, dma, dma, dma, dma, dma((NZ,)), dma,
            dma, dma, dma, dma, dma, dma((NZ,)), dma,
        ],
        compiler_params=pltpu.CompilerParams(
            collective_id=0, has_side_effects=True, vmem_limit_bytes=48 * 1024 * 1024
        ),
    )(
        queries,
        keys.reshape(blocks, BLK, HD),
        values.reshape(blocks, BLK, HD),
        vertical, slash_blocks, slash_count, row_order,
    )


def solution(mesh):
    in_specs = (
        P(("ctx", "kvh"), None),
        P("kvh", "ctx", None),
        P("kvh", "ctx", None),
        P("kvh", None),
        P("kvh", "ctx", None),
        P("kvh", "ctx"),
        P("kvh", "ctx"),
    )
    out_specs = P(("ctx", "kvh"), None)
    return jax.shard_map(
        per_device, mesh=mesh, in_specs=in_specs, out_specs=out_specs, check_vma=False
    )
```

```python
import math

import jax
import jax.numpy as jnp
from jax import lax
from jax.experimental import pallas as pl
from jax.experimental.pallas import tpu as pltpu
from jax.sharding import PartitionSpec as P

MESH = pl.DeviceIdType.MESH
BLK = 64
HD = 128
QH = 8
NY = 8
NZ = 8
NCTX = NY * NZ
NKV = 8
WIDTH = QH * HD
TOK = 16
SMAX = 32
STAT = WIDTH + 128
NEG = -1e30
SCALE2 = math.log2(math.e) / math.sqrt(HD)
LOG2E = math.log2(math.e)
ROUTES = ((0, 0, 2, (0, 1)), (-1, 2, 2, (0, 1)), (1, 4, 2, (0, 1)), (-2, 6, 1, (0,)), (2, 7, 1, (1,)))


def wait_for(ref, sem):
    pltpu.make_async_copy(ref, ref, sem).wait()


def kernel(
    q_ref, k_ref, v_ref, vert_ref, lists_ref, cnt_ref, ord_ref, out_ref,
    kbuf, vbuf, mrow, mall, msm, pickv, picks, qbuf, q2, gath, stag, kv, va, vb, vc,
    acc, mx, ls, bias, ostage, orecv,
    lsem, s_meta, s_q, s_va, s_vb, s_vc, s_y, s_z, s_out,
    r_meta, r_q, r_va, r_vb, r_vc, r_y, r_z, r_out,
):
    me = lax.axis_index("ctx")
    h = lax.axis_index("kvh")
    y, z = me // NZ, me % NZ

    def at(yy, zz):
        return lax.rem(yy + 2 * NY, NY) * NZ + lax.rem(zz + 2 * NZ, NZ)

    def push(src, dst, ssem, rsem, ctx, kvh):
        pltpu.make_async_remote_copy(
            src_ref=src, dst_ref=dst, send_sem=ssem, recv_sem=rsem,
            device_id=(ctx, kvh), device_id_type=MESH,
        ).start()

    load_k = pltpu.make_async_copy(k_ref, kbuf, lsem.at[0])
    load_v = pltpu.make_async_copy(v_ref, vbuf, lsem.at[1])
    load_k.start()
    load_v.start()

    homes = (at(y + 2, z), at(y - 2, z))

    barrier = pltpu.get_barrier_semaphore()
    for t in range(1, NZ):
        pl.semaphore_signal(barrier, inc=1, device_id=(at(y, z + t), h), device_id_type=MESH)
    for t in range(1, NY):
        pl.semaphore_signal(barrier, inc=1, device_id=(at(y + t, z), h), device_id_type=MESH)
    for home in homes:
        for t in range(1, NKV):
            pl.semaphore_signal(
                barrier, inc=1, device_id=(home, lax.rem(h + t, NKV)), device_id_type=MESH
            )

    lane = lax.broadcasted_iota(jnp.int32, (1, 128), 1)
    mrow[0] = jnp.full((1, 128), -1, jnp.int32)
    mrow[0, :, 0:SMAX] = lists_ref[0, 0:1, :]
    mrow[0, :, SMAX:2 * SMAX] = lists_ref[0, 1:2, :]
    row = mrow[0]
    limit = jnp.where(lane < SMAX, cnt_ref[0, 0], cnt_ref[0, 1] + SMAX)
    row = jnp.where(lane < limit, row, -1)
    row = jnp.where(lane == 2 * SMAX, ord_ref[0, 0], row)
    row = jnp.where(lane == 2 * SMAX + 1, ord_ref[0, 1], row)
    mall[me] = row

    pl.semaphore_wait(barrier, NZ - 1 + NY - 1 + 2 * (NKV - 1))

    for t in range(1, NZ):
        push(mall.at[me], mall.at[me], s_meta.at[0], r_meta.at[0], at(y, z + t), h)

    token_rows = pl.ds(pl.multiple_of(lax.rem(h, 4) * TOK, TOK), TOK)

    def send_queries(where):
        for t in range(NKV):
            push(
                q_ref.at[:, pl.ds(t * WIDTH, WIDTH)],
                qbuf.at[where * 2 + h // 4, token_rows, :],
                s_q.at[where], r_q.at[where], homes[1 - where], t,
            )

    wait_for(mall.at[pl.ds(0, NZ - 1)], r_meta.at[0])
    my_row = pl.ds(pl.multiple_of(y * NZ, NZ), NZ)
    for t in range(1, NY):
        push(mall.at[my_row], mall.at[my_row], s_meta.at[1], r_meta.at[1], at(y + t, z), h)

    send_queries(0)

    load_k.wait()
    load_v.wait()
    mine = jnp.int32(0)
    for i in range(NKV):
        entry = vert_ref[0, i]
        mine = jnp.where(entry // 32 == me, lax.rem(entry, 32), mine)
    va[0, 0] = kbuf[mine]
    va[0, 1] = vbuf[mine]

    wait_for(mall.at[pl.ds(0, NCTX - NZ)], r_meta.at[1])
    to_msm = [
        pltpu.make_async_copy(mall.at[homes[i]], msm.at[i], lsem.at[3 + i]) for i in range(2)
    ]
    for copy in to_msm:
        copy.start()
    low = mall[0:NCTX // 2].reshape(NCTX // 2, 128)
    high = mall[NCTX // 2:NCTX].reshape(NCTX // 2, 128)
    wide = lax.broadcasted_iota(jnp.int32, (NCTX // 2, 128), 1)
    entries = jnp.where(wide < 2 * SMAX, low, pltpu.roll(high, 2 * SMAX, 1))
    own = lax.shift_right_arithmetic(entries, 5) == me
    local = entries & 31
    first = jnp.min(jnp.where(own, local, 99), axis=1, keepdims=True)
    last = jnp.max(jnp.where(own, local, 0), axis=1, keepdims=True)
    first = jnp.where(first == 99, 0, first)
    pickv[...] = jnp.where(wide == 0, first, last)
    to_picks = pltpu.make_async_copy(pickv, picks, lsem.at[2])
    to_picks.start()
    to_picks.wait()

    def send_y(dz):
        for dy, start, count, which in ROUTES:
            pair = lax.rem(y + dy + 2 + NY, 4) * NZ + lax.rem(z + dz, NZ)
            for i in range(count):
                pick = picks[pair, which[i]]
                if dy == 0:
                    stag[dz, start + i, 0] = kbuf[pick]
                    stag[dz, start + i, 1] = vbuf[pick]
                else:
                    gath[dz, start + i - 2, 0] = kbuf[pick]
                    gath[dz, start + i - 2, 1] = vbuf[pick]
            if dy != 0:
                push(
                    gath.at[dz, pl.ds(start - 2, count)], stag.at[dz, pl.ds(start, count)],
                    s_y.at[dz], r_y.at[dz], at(y + dy, z), h,
                )

    def send_z(dz):
        wait_for(stag.at[dz, pl.ds(2, 6)], r_y.at[dz])
        push(stag.at[dz], kv.at[dz], s_z.at[dz], r_z.at[dz], at(y, z + dz), h)

    send_y(1)
    send_y(7)
    send_y(2)
    send_y(6)
    send_queries(1)
    send_z(1)
    send_z(7)
    for a in range(1, NY):
        push(va.at[0], va.at[a], s_va, r_va, at(y + a, z), h)
    send_y(3)
    send_y(5)
    send_y(4)
    send_y(0)

    for copy in to_msm:
        copy.wait()
    slot = lax.broadcasted_iota(jnp.int32, (NZ, 8 * BLK), 1) // BLK
    back = lax.broadcasted_iota(jnp.int32, (NZ, 8 * BLK), 0)
    step = jnp.where(slot < 2, 0, jnp.where(slot < 4, 1, jnp.where(slot < 6, -1, jnp.where(slot == 6, 2, -2))))
    source = ((y + step) & (NY - 1)) * NZ + ((z - back) & (NZ - 1))

    def scan(t, carry):
        lo, hi = carry
        for i in range(2):
            entry = msm[i, 0, t]
            hit = source == lax.shift_right_arithmetic(entry, 5)
            lo = jnp.where(hit, jnp.minimum(lo, entry), lo)
            hi = jnp.where(hit, jnp.maximum(hi, entry), hi)
        return lo, hi

    lo, hi = lax.fori_loop(
        0, 2 * SMAX, scan,
        (jnp.full((NZ, 8 * BLK), 1 << 20, jnp.int32), jnp.full((NZ, 8 * BLK), -3, jnp.int32)),
    )
    second = (slot == 1) | (slot == 3) | (slot == 5) | (slot == 7)
    held = jnp.where(second, jnp.where(hi > lo, hi, -2), lo)

    stay = msm[0, 0, 2 * SMAX] & 1
    came = msm[0, 0, 2 * SMAX + 1] & 1
    source_block = (stay, 2 + came, 3 - came, 1 - stay)
    for r in range(4):
        block = source_block[r]
        side = block // 2
        first_entry = lax.rem(block, 2) * SMAX

        def member(t, need, side=side, first_entry=first_entry):
            return need | (held == msm[side, 0, first_entry + t]).astype(jnp.int32)

        need = lax.fori_loop(0, SMAX, member, jnp.zeros((NZ, 8 * BLK), jnp.int32))
        bias[r] = jnp.where(need > 0, 0.0, NEG)

    send_z(2)
    send_z(6)

    for i in range(8):
        acc[i] = jnp.zeros((256, HD), jnp.float32)
        ls[i] = jnp.zeros((256, 128), jnp.float32)
        mx[i] = jnp.full((256, 128), NEG, jnp.float32)

    owner = vert_ref[0, y] // 32
    near = lax.rem(y - owner // NZ + NY, NY)
    wait_for(va.at[pl.ds(1, NY - 1)], r_va)
    vb[0] = va[near]
    for b in range(1, NZ):
        push(vb.at[0], vb.at[b], s_vb, r_vb, at(y, z + b), h)

    for where in range(2):
        wait_for(qbuf.at[pl.ds(where * 2, 2)], r_q.at[where])
    for r in range(4):
        for g in range(QH):
            q2[r * 2 + g // 4, pl.ds((g % 4) * BLK, BLK), :] = qbuf[
                source_block[r], :, pl.ds(g * HD, HD)
            ]

    send_z(3)
    send_z(5)

    def attend_rows(r, load, size, dz):
        tiles = (2 * r, 2 * r + 1)
        keys, values = load()
        scores = [
            lax.dot_general(
                q2[i], keys, (((1,), (1,)), ((), ())), preferred_element_type=jnp.float32
            )
            for i in tiles
        ]
        if dz is not None:
            extra = bias[r, dz:dz + 1, :]
            scores = [s + extra for s in scores]
        old = [mx[i] for i in tiles]
        new = [jnp.maximum(o, jnp.max(s, axis=1, keepdims=True)) for o, s in zip(old, scores)]
        shrink = [jnp.exp2((o - n) * SCALE2) for o, n in zip(old, new)]
        weights = [
            jnp.exp2(s * SCALE2 - jnp.concatenate([n * SCALE2] * (size // 128), axis=1))
            for s, n in zip(scores, new)
        ]
        for k, i in enumerate(tiles):
            total = weights[k][:, 0:128]
            for j in range(1, size // 128):
                total = total + weights[k][:, j * 128:(j + 1) * 128]
            ls[i] = ls[i] * shrink[k] + total
            acc[i] = acc[i] * shrink[k] + jnp.dot(
                weights[k].astype(jnp.bfloat16), values, preferred_element_type=jnp.float32
            )
            mx[i] = new[k]

    def attend(load, size, dz):
        def body(r, _):
            attend_rows(r, load, size, dz)
            return 0

        lax.fori_loop(0, 4, body, 0)

    def chunk(dz):
        buf = stag if dz == 0 else kv

        def load():
            return buf[dz, :, 0].reshape(8 * BLK, HD), buf[dz, :, 1].reshape(8 * BLK, HD)

        if dz == 0:
            wait_for(stag.at[0, pl.ds(2, 6)], r_y.at[0])
        else:
            wait_for(kv.at[dz], r_z.at[dz])
        return load, 8 * BLK, dz

    attend(*chunk(1))

    near = lax.rem(z - lax.rem(owner, NZ) + NZ, NZ)
    wait_for(vb.at[pl.ds(1, NZ - 1)], r_vb)
    index = lax.rem(y, 4)
    vc[index] = vb[near]
    for t in range(1, 4):
        push(
            vc.at[index], vc.at[index], s_vc, r_vc,
            at((y // 4) * 4 + lax.rem(index + t, 4), z), h,
        )
    send_z(4)

    attend(*chunk(7))
    attend(*chunk(0))
    attend(*chunk(2))
    attend(*chunk(6))
    wait_for(vc.at[pl.ds(0, 3)], r_vc)
    attend(
        lambda: (vc[:, 0].reshape(4 * BLK, HD), vc[:, 1].reshape(4 * BLK, HD)), 4 * BLK, None
    )
    attend(*chunk(3))
    attend(*chunk(5))
    last_chunk = chunk(4)

    lanes = lax.broadcasted_iota(jnp.int32, (BLK, 128), 1)

    def finish(r):
        stats = jnp.zeros((BLK, 128), jnp.float32)
        for half in range(2):
            i = r * 2 + half
            total = jnp.sum(ls[i], axis=1, keepdims=True)
            mixed = acc[i] / total
            weight = mx[i] * SCALE2 + jnp.log(total) * LOG2E
            big = weight.astype(jnp.bfloat16).astype(jnp.float32)
            rest = weight - big
            mid = rest.astype(jnp.bfloat16).astype(jnp.float32)
            tail = rest - mid
            for j in range(4):
                g = half * 4 + j
                rows = slice(j * BLK, (j + 1) * BLK)
                ostage[r, :, g * HD:(g + 1) * HD] = mixed[rows].astype(jnp.bfloat16)
                stats = jnp.where(lanes == g, big[rows], stats)
                stats = jnp.where(lanes == QH + g, mid[rows], stats)
                stats = jnp.where(lanes == 2 * QH + g, tail[rows], stats)
        ostage[r, :, WIDTH:STAT] = stats.astype(jnp.bfloat16)

    for r in (0, 2, 1, 3):
        attend_rows(r, *last_chunk)
        finish(r)
        for t in range(4):
            push(
                ostage.at[r, pl.ds(t * TOK, TOK), :], orecv.at[r // 2, h],
                s_out, r_out.at[h], homes[r // 2], (r % 2) * 4 + t,
            )

    for head in range(NKV):
        wait_for(orecv.at[:, head], r_out.at[head])
        logs = []
        for i in range(2):
            terms = orecv[i, head, :, WIDTH:STAT].astype(jnp.float32)
            logs.append(terms + pltpu.roll(terms, 128 - QH, 1) + pltpu.roll(terms, 128 - 2 * QH, 1))
        share = 1.0 / (1.0 + jnp.exp2(logs[1] - logs[0]))
        for g in range(QH):
            cols = slice(g * HD, (g + 1) * HD)
            part = share[:, g:g + 1]
            one = orecv[0, head, :, cols].astype(jnp.float32)
            two = orecv[1, head, :, cols].astype(jnp.float32)
            out_ref[:, head * WIDTH + g * HD:head * WIDTH + (g + 1) * HD] = (
                one * part + two * (1.0 - part)
            ).astype(jnp.bfloat16)

    wait_for(mall.at[pl.ds(0, NZ - 1)], s_meta.at[0])
    wait_for(mall.at[pl.ds(0, NCTX - NZ)], s_meta.at[1])
    for where in range(2):
        wait_for(qbuf.at[pl.ds(where * 2, 2)], s_q.at[where])
    wait_for(va.at[pl.ds(1, NY - 1)], s_va)
    wait_for(vb.at[pl.ds(1, NZ - 1)], s_vb)
    wait_for(vc.at[pl.ds(0, 3)], s_vc)
    for dz in range(NZ):
        wait_for(gath.at[dz], s_y.at[dz])
    for dz in range(1, NZ):
        wait_for(stag.at[dz], s_z.at[dz])
    wait_for(ostage, s_out)


def per_device(queries, keys, values, vertical, slash_blocks, slash_count, row_order):
    bf16, f32, i32 = jnp.bfloat16, jnp.float32, jnp.int32
    blocks = keys.shape[1] // BLK
    vmem = pltpu.VMEM
    dma = pltpu.SemaphoreType.DMA
    hbm_spec = pl.BlockSpec(memory_space=pltpu.HBM)
    vmem_spec = pl.BlockSpec(memory_space=pltpu.VMEM)
    smem_spec = pl.BlockSpec(memory_space=pltpu.SMEM)
    return pl.pallas_call(
        kernel,
        out_shape=jax.ShapeDtypeStruct(queries.shape, bf16),
        in_specs=[hbm_spec, hbm_spec, hbm_spec, smem_spec, vmem_spec, smem_spec, smem_spec],
        out_specs=vmem_spec,
        scratch_shapes=[
            vmem((blocks, BLK, HD), bf16),
            vmem((blocks, BLK, HD), bf16),
            vmem((1, 1, 128), i32),
            vmem((NCTX, 1, 128), i32),
            pltpu.SMEM((2, 1, 128), i32),
            vmem((NCTX // 2, 128), i32),
            pltpu.SMEM((NCTX // 2, 128), i32),
            vmem((4, BLK, WIDTH), bf16),
            vmem((8, 256, HD), bf16),
            vmem((NZ, 6, 2, BLK, HD), bf16),
            vmem((NZ, 8, 2, BLK, HD), bf16),
            vmem((NZ, 8, 2, BLK, HD), bf16),
            vmem((NY, 2, BLK, HD), bf16),
            vmem((NZ, 2, BLK, HD), bf16),
            vmem((4, 2, BLK, HD), bf16),
            vmem((8, 256, HD), f32),
            vmem((8, 256, 128), f32),
            vmem((8, 256, 128), f32),
            vmem((4, NZ, 8 * BLK), f32),
            vmem((4, BLK, STAT), bf16),
            vmem((2, NKV, TOK, STAT), bf16),
            dma((5,)),
            dma((2,)), dma((2,)), dma, dma, dma, dma((NZ,)), dma((NZ,)), dma,
            dma((2,)), dma((2,)), dma, dma, dma, dma((NZ,)), dma((NZ,)), dma((NKV,)),
        ],
        compiler_params=pltpu.CompilerParams(
            collective_id=0, has_side_effects=True, vmem_limit_bytes=60 * 1024 * 1024
        ),
    )(
        queries,
        keys.reshape(blocks, BLK, HD),
        values.reshape(blocks, BLK, HD),
        vertical, slash_blocks, slash_count, row_order,
    )


def solution(mesh):
    in_specs = (
        P(("ctx", "kvh"), None),
        P("kvh", "ctx", None),
        P("kvh", "ctx", None),
        P("kvh", None),
        P("kvh", "ctx", None),
        P("kvh", "ctx"),
        P("kvh", "ctx"),
    )
    out_specs = P(("ctx", "kvh"), None)
    return jax.shard_map(
        per_device, mesh=mesh, in_specs=in_specs, out_specs=out_specs, check_vma=False
    )
```

```python
import math

import jax
import jax.numpy as jnp
from jax import lax
from jax.experimental import pallas as pl
from jax.experimental.pallas import tpu as pltpu
from jax.sharding import PartitionSpec as P

MESH = pl.DeviceIdType.MESH
BLK = 64
HD = 128
QH = 8
NY = 8
NZ = 8
NCTX = NY * NZ
NKV = 8
WIDTH = QH * HD
TOK = 16
SMAX = 32
NEG = -1e30
SCALE2 = math.log2(math.e) / math.sqrt(HD)
LOG2E = math.log2(math.e)
ROUTES = ((0, 0, 2, (0, 1)), (-1, 2, 2, (0, 1)), (1, 4, 2, (0, 1)), (-2, 6, 1, (0,)), (2, 7, 1, (1,)))


def wait_for(ref, sem):
    pltpu.make_async_copy(ref, ref, sem).wait()


def kernel(
    q_ref, k_ref, v_ref, vert_ref, lists_ref, cnt_ref, ord_ref, out_ref,
    kbuf, vbuf, mrow, mall, msm, pickv, picks, qbuf, q2, gath, stag, kv, va, vb, vsrc, vc,
    acc, mx, ls, bias, ostage, orecv, lstage, lrecv,
    lsem, s_meta, s_q, s_va, s_vb, s_vc, s_y, s_z, s_out, s_stat,
    r_meta, r_q, r_va, r_vb, r_vc, r_y, r_z, r_out, r_stat,
):
    me = lax.axis_index("ctx")
    h = lax.axis_index("kvh")
    y, z = me // NZ, me % NZ

    def at(yy, zz):
        return lax.rem(yy + 2 * NY, NY) * NZ + lax.rem(zz + 2 * NZ, NZ)

    def push(src, dst, ssem, rsem, ctx, kvh):
        pltpu.make_async_remote_copy(
            src_ref=src, dst_ref=dst, send_sem=ssem, recv_sem=rsem,
            device_id=(ctx, kvh), device_id_type=MESH,
        ).start()

    load_k = pltpu.make_async_copy(k_ref, kbuf, lsem.at[0])
    load_v = pltpu.make_async_copy(v_ref, vbuf, lsem.at[1])
    load_k.start()
    load_v.start()

    homes = (at(y + 2, z), at(y - 2, z))

    barrier = pltpu.get_barrier_semaphore()
    for t in range(1, NZ):
        pl.semaphore_signal(barrier, inc=1, device_id=(at(y, z + t), h), device_id_type=MESH)
    for t in range(1, NY):
        pl.semaphore_signal(barrier, inc=1, device_id=(at(y + t, z), h), device_id_type=MESH)
    for home in homes:
        for t in range(1, NKV):
            pl.semaphore_signal(
                barrier, inc=1, device_id=(home, lax.rem(h + t, NKV)), device_id_type=MESH
            )

    lane = lax.broadcasted_iota(jnp.int32, (1, 128), 1)
    mrow[0] = jnp.full((1, 128), -1, jnp.int32)
    mrow[0, :, 0:SMAX] = lists_ref[0, 0:1, :]
    mrow[0, :, SMAX:2 * SMAX] = lists_ref[0, 1:2, :]
    row = mrow[0]
    limit = jnp.where(lane < SMAX, cnt_ref[0, 0], cnt_ref[0, 1] + SMAX)
    row = jnp.where(lane < limit, row, -1)
    row = jnp.where(lane == 2 * SMAX, ord_ref[0, 0], row)
    row = jnp.where(lane == 2 * SMAX + 1, ord_ref[0, 1], row)
    mall[me] = row

    pl.semaphore_wait(barrier, NZ - 1 + NY - 1 + 2 * (NKV - 1))

    for t in range(1, NZ):
        push(mall.at[me], mall.at[me], s_meta.at[0], r_meta.at[0], at(y, z + t), h)

    token_rows = pl.ds(pl.multiple_of(lax.rem(h, 4) * TOK, TOK), TOK)

    def send_queries(where):
        for i in range(NKV):
            t = lax.rem(h + i, NKV)
            push(
                q_ref.at[:, pl.ds(pl.multiple_of(t * WIDTH, WIDTH), WIDTH)],
                qbuf.at[where * 2 + h // 4, token_rows, :],
                s_q.at[where], r_q.at[where], homes[1 - where], t,
            )

    wait_for(mall.at[pl.ds(0, NZ - 1)], r_meta.at[0])
    my_row = pl.ds(pl.multiple_of(y * NZ, NZ), NZ)
    for t in range(1, NY):
        push(mall.at[my_row], mall.at[my_row], s_meta.at[1], r_meta.at[1], at(y + t, z), h)

    load_k.wait()
    load_v.wait()
    mine = jnp.int32(0)
    for i in range(NKV):
        entry = vert_ref[0, i]
        mine = jnp.where(entry // 32 == me, lax.rem(entry, 32), mine)
    va[0, 0] = kbuf[mine]
    va[0, 1] = vbuf[mine]
    for b in range(1, NZ):
        push(va.at[0], va.at[b], s_va, r_va, at(y, z + b), h)

    wait_for(mall.at[pl.ds(0, NCTX - NZ)], r_meta.at[1])
    to_msm = [
        pltpu.make_async_copy(mall.at[homes[i]], msm.at[i], lsem.at[3 + i]) for i in range(2)
    ]
    for copy in to_msm:
        copy.start()
    low = mall[0:NCTX // 2].reshape(NCTX // 2, 128)
    high = mall[NCTX // 2:NCTX].reshape(NCTX // 2, 128)
    wide = lax.broadcasted_iota(jnp.int32, (NCTX // 2, 128), 1)
    entries = jnp.where(wide < 2 * SMAX, low, pltpu.roll(high, 2 * SMAX, 1))
    own = lax.shift_right_arithmetic(entries, 5) == me
    local = entries & 31
    first = jnp.min(jnp.where(own, local, 99), axis=1, keepdims=True)
    last = jnp.max(jnp.where(own, local, 0), axis=1, keepdims=True)
    first = jnp.where(first == 99, 0, first)
    pickv[...] = jnp.where(wide == 0, first, last)
    to_picks = pltpu.make_async_copy(pickv, picks, lsem.at[2])
    to_picks.start()
    to_picks.wait()

    def send_y(dz):
        for dy, start, count, which in ROUTES:
            pair = lax.rem(y + dy + 2 + NY, 4) * NZ + lax.rem(z + dz, NZ)
            for i in range(count):
                pick = picks[pair, which[i]]
                if dy == 0:
                    stag[dz, start + i, 0] = kbuf[pick]
                    stag[dz, start + i, 1] = vbuf[pick]
                else:
                    gath[dz, start + i - 2, 0] = kbuf[pick]
                    gath[dz, start + i - 2, 1] = vbuf[pick]
            if dy == 0 and dz != 0:
                push(
                    stag.at[dz, pl.ds(0, 2)], kv.at[dz, pl.ds(0, 2)],
                    s_z.at[dz], r_z.at[dz], at(y, z + dz), h,
                )
            if dy != 0:
                push(
                    gath.at[dz, pl.ds(start - 2, count)], stag.at[dz, pl.ds(start, count)],
                    s_y.at[dz], r_y.at[dz], at(y + dy, z), h,
                )

    def send_z(dz):
        wait_for(stag.at[dz, pl.ds(2, 6)], r_y.at[dz])
        push(
            stag.at[dz, pl.ds(2, 6)], kv.at[dz, pl.ds(2, 6)],
            s_z.at[dz], r_z.at[dz], at(y, z + dz), h,
        )

    for dz in (4, 3, 5):
        send_y(dz)
    send_queries(0)
    send_queries(1)
    for dz in (2, 6):
        send_y(dz)
    for dz in (4, 3, 5):
        send_z(dz)

    owner = vert_ref[0, z] // 32
    wait_for(va.at[pl.ds(1, NZ - 1)], r_va)
    vb[0] = va[lax.rem(z - lax.rem(owner, NZ) + NZ, NZ)]
    for a in range(1, NY):
        push(vb.at[0], vb.at[a], s_vb, r_vb, at(y + a, z), h)

    for dz in (1, 7, 0):
        send_y(dz)

    for copy in to_msm:
        copy.wait()
    slot = lax.broadcasted_iota(jnp.int32, (NZ, 8 * BLK), 1) // BLK
    back = lax.broadcasted_iota(jnp.int32, (NZ, 8 * BLK), 0)
    step = jnp.where(slot < 2, 0, jnp.where(slot < 4, 1, jnp.where(slot < 6, -1, jnp.where(slot == 6, 2, -2))))
    source = ((y + step) & (NY - 1)) * NZ + ((z - back) & (NZ - 1))

    def scan(t, carry):
        lo, hi = carry
        for i in range(2):
            entry = msm[i, 0, t]
            hit = source == lax.shift_right_arithmetic(entry, 5)
            lo = jnp.where(hit, jnp.minimum(lo, entry), lo)
            hi = jnp.where(hit, jnp.maximum(hi, entry), hi)
        return lo, hi

    lo, hi = lax.fori_loop(
        0, 2 * SMAX, scan,
        (jnp.full((NZ, 8 * BLK), 1 << 20, jnp.int32), jnp.full((NZ, 8 * BLK), -3, jnp.int32)),
    )
    second = (slot == 1) | (slot == 3) | (slot == 5) | (slot == 7)
    held = jnp.where(second, jnp.where(hi > lo, hi, -2), lo)

    stay = msm[0, 0, 2 * SMAX] & 1
    came = msm[0, 0, 2 * SMAX + 1] & 1
    source_block = (stay, 2 + came, 3 - came, 1 - stay)
    for r in range(4):
        block = source_block[r]
        side = block // 2
        first_entry = lax.rem(block, 2) * SMAX

        def member(t, need, side=side, first_entry=first_entry):
            return need | (held == msm[side, 0, first_entry + t]).astype(jnp.int32)

        need = lax.fori_loop(0, SMAX, member, jnp.zeros((NZ, 8 * BLK), jnp.int32))
        bias[r] = jnp.where(need > 0, 0.0, NEG)

    for i in range(8):
        acc[i] = jnp.zeros((256, HD), jnp.float32)
        ls[i] = jnp.zeros((256, 128), jnp.float32)
        mx[i] = jnp.full((256, 128), NEG, jnp.float32)

    send_z(2)
    send_z(6)

    upper = y // 4
    wait_for(vb.at[pl.ds(1, NY - 1)], r_vb)
    vsrc[...] = vb[lax.rem(y - owner // NZ + NY, NY)]
    for j, (low_step, high_step) in enumerate(((0, 4), (1, 3), (-1, -3), (2, -2))):
        target = at(y, z - jnp.where(upper == 1, high_step, low_step))
        if j == 0:
            @pl.when(upper == 0)
            def _():
                vc[0] = vsrc[...]

            @pl.when(upper == 1)
            def _(target=target):
                push(vsrc, vc.at[0], s_vc, r_vc, target, h)
        else:
            push(vsrc, vc.at[j], s_vc, r_vc, target, h)

    for where in range(2):
        wait_for(qbuf.at[pl.ds(where * 2, 2)], r_q.at[where])
    for r in range(4):
        for g in range(QH):
            q2[r * 2 + g // 4, pl.ds((g % 4) * BLK, BLK), :] = qbuf[
                source_block[r], :, pl.ds(g * HD, HD)
            ]

    def attend_rows(r, load, size, dz):
        tiles = (2 * r, 2 * r + 1)
        keys, values = load()
        scores = [
            lax.dot_general(
                q2[i], keys, (((1,), (1,)), ((), ())), preferred_element_type=jnp.float32
            )
            for i in tiles
        ]
        if dz is not None:
            extra = bias[r, dz:dz + 1, :]
            scores = [s + extra for s in scores]
        old = [mx[i] for i in tiles]
        new = [jnp.maximum(o, jnp.max(s, axis=1, keepdims=True)) for o, s in zip(old, scores)]
        shrink = [jnp.exp2((o - n) * SCALE2) for o, n in zip(old, new)]
        weights = [
            jnp.exp2(s * SCALE2 - jnp.concatenate([n * SCALE2] * (size // 128), axis=1))
            for s, n in zip(scores, new)
        ]
        for k, i in enumerate(tiles):
            total = weights[k][:, 0:128]
            for j in range(1, size // 128):
                total = total + weights[k][:, j * 128:(j + 1) * 128]
            ls[i] = ls[i] * shrink[k] + total
            acc[i] = acc[i] * shrink[k] + jnp.dot(
                weights[k].astype(jnp.bfloat16), values, preferred_element_type=jnp.float32
            )
            mx[i] = new[k]

    def attend(load, size, dz):
        def body(r, _):
            attend_rows(r, load, size, dz)
            return 0

        lax.fori_loop(0, 4, body, 0)

    def chunk(dz):
        buf = stag if dz == 0 else kv

        def load():
            return buf[dz, :, 0].reshape(8 * BLK, HD), buf[dz, :, 1].reshape(8 * BLK, HD)

        if dz == 0:
            wait_for(stag.at[0, pl.ds(2, 6)], r_y.at[0])
        else:
            wait_for(kv.at[dz], r_z.at[dz])
        return load, 8 * BLK, dz

    attend(*chunk(4))
    send_z(1)
    send_z(7)
    attend(*chunk(3))
    attend(*chunk(5))
    attend(*chunk(0))
    attend(*chunk(2))
    attend(*chunk(6))

    def wait_vertical(sem):
        @pl.when(upper == 0)
        def _():
            wait_for(vc.at[pl.ds(0, 3)], sem)

        @pl.when(upper == 1)
        def _():
            wait_for(vc, sem)

    wait_vertical(r_vc)
    attend(
        lambda: (vc[:, 0].reshape(4 * BLK, HD), vc[:, 1].reshape(4 * BLK, HD)), 4 * BLK, None
    )
    last_chunks = chunk(1), chunk(7)

    lanes = lax.broadcasted_iota(jnp.int32, (BLK, 128), 1)
    spot = lax.broadcasted_iota(jnp.int32, (BLK, 128), 0) & (TOK - 1)

    def finish(r):
        stats = jnp.zeros((BLK, 128), jnp.float32)
        for half in range(2):
            i = r * 2 + half
            total = jnp.sum(ls[i], axis=1, keepdims=True)
            mixed = acc[i] / total
            weight = mx[i] * SCALE2 + jnp.log(total) * LOG2E
            for j in range(4):
                g = half * 4 + j
                rows = slice(j * BLK, (j + 1) * BLK)
                ostage[r, :, g * HD:(g + 1) * HD] = mixed[rows].astype(jnp.bfloat16)
                stats = jnp.where(lanes == g * TOK + spot, weight[rows], stats)
        for t in range(4):
            lstage[r, t] = jnp.sum(stats[t * TOK:(t + 1) * TOK], axis=0, keepdims=True)

    for i in range(4):
        r = (i % 2) * 2 + ((i // 2) ^ ((h // 2) & 1))
        home = homes[i % 2]
        for last in last_chunks:
            attend_rows(r, *last)
        finish(r)
        for k in range(4):
            t = lax.rem(h + k, 4)
            token_device = lax.rem(r, 2) * 4 + t
            push(
                ostage.at[r, pl.ds(pl.multiple_of(t * TOK, TOK), TOK), :], orecv.at[i % 2, h],
                s_out, r_out.at[h], home, token_device,
            )
            push(
                lstage.at[r, t], lrecv.at[i % 2, h], s_stat, r_stat.at[h],
                home, token_device,
            )

    for head in range(NKV):
        wait_for(orecv.at[:, head], r_out.at[head])
        wait_for(lrecv.at[:, head], r_stat.at[head])
        share = 1.0 / (1.0 + jnp.exp2(lrecv[1, head] - lrecv[0, head]))
        share = jnp.broadcast_to(share, (TOK, 128))
        for g in range(QH):
            cols = slice(g * HD, (g + 1) * HD)
            part = jnp.sum(
                jnp.where(lanes[:TOK] == g * TOK + spot[:TOK], share, 0.0), axis=1, keepdims=True
            )
            one = orecv[0, head, :, cols].astype(jnp.float32)
            two = orecv[1, head, :, cols].astype(jnp.float32)
            out_ref[:, head * WIDTH + g * HD:head * WIDTH + (g + 1) * HD] = (
                one * part + two * (1.0 - part)
            ).astype(jnp.bfloat16)

    wait_for(mall.at[pl.ds(0, NZ - 1)], s_meta.at[0])
    wait_for(mall.at[pl.ds(0, NCTX - NZ)], s_meta.at[1])
    for where in range(2):
        wait_for(qbuf.at[pl.ds(where * 2, 2)], s_q.at[where])
    wait_for(va.at[pl.ds(1, NY - 1)], s_va)
    wait_for(vb.at[pl.ds(1, NZ - 1)], s_vb)
    wait_vertical(s_vc)
    for dz in range(NZ):
        wait_for(gath.at[dz], s_y.at[dz])
    for dz in range(1, NZ):
        wait_for(stag.at[dz], s_z.at[dz])
    wait_for(ostage, s_out)
    wait_for(lstage, s_stat)


def per_device(queries, keys, values, vertical, slash_blocks, slash_count, row_order):
    bf16, f32, i32 = jnp.bfloat16, jnp.float32, jnp.int32
    blocks = keys.shape[1] // BLK
    vmem = pltpu.VMEM
    dma = pltpu.SemaphoreType.DMA
    hbm_spec = pl.BlockSpec(memory_space=pltpu.HBM)
    vmem_spec = pl.BlockSpec(memory_space=pltpu.VMEM)
    smem_spec = pl.BlockSpec(memory_space=pltpu.SMEM)
    return pl.pallas_call(
        kernel,
        out_shape=jax.ShapeDtypeStruct(queries.shape, bf16),
        in_specs=[hbm_spec, hbm_spec, hbm_spec, smem_spec, vmem_spec, smem_spec, smem_spec],
        out_specs=vmem_spec,
        scratch_shapes=[
            vmem((blocks, BLK, HD), bf16),
            vmem((blocks, BLK, HD), bf16),
            vmem((1, 1, 128), i32),
            vmem((NCTX, 1, 128), i32),
            pltpu.SMEM((2, 1, 128), i32),
            vmem((NCTX // 2, 128), i32),
            pltpu.SMEM((NCTX // 2, 128), i32),
            vmem((4, BLK, WIDTH), bf16),
            vmem((8, 256, HD), bf16),
            vmem((NZ, 6, 2, BLK, HD), bf16),
            vmem((NZ, 8, 2, BLK, HD), bf16),
            vmem((NZ, 8, 2, BLK, HD), bf16),
            vmem((NY, 2, BLK, HD), bf16),
            vmem((NZ, 2, BLK, HD), bf16),
            vmem((2, BLK, HD), bf16),
            vmem((4, 2, BLK, HD), bf16),
            vmem((8, 256, HD), f32),
            vmem((8, 256, 128), f32),
            vmem((8, 256, 128), f32),
            vmem((4, NZ, 8 * BLK), f32),
            vmem((4, BLK, WIDTH), bf16),
            vmem((2, NKV, TOK, WIDTH), bf16),
            vmem((4, 4, 1, 128), f32),
            vmem((2, NKV, 1, 128), f32),
            dma((5,)),
            dma((2,)), dma((2,)), dma, dma, dma, dma((NZ,)), dma((NZ,)), dma, dma,
            dma((2,)), dma((2,)), dma, dma, dma, dma((NZ,)), dma((NZ,)), dma((NKV,)), dma((NKV,)),
        ],
        compiler_params=pltpu.CompilerParams(
            collective_id=0, has_side_effects=True, vmem_limit_bytes=60 * 1024 * 1024
        ),
    )(
        queries,
        keys.reshape(blocks, BLK, HD),
        values.reshape(blocks, BLK, HD),
        vertical, slash_blocks, slash_count, row_order,
    )


def solution(mesh):
    in_specs = (
        P(("ctx", "kvh"), None),
        P("kvh", "ctx", None),
        P("kvh", "ctx", None),
        P("kvh", None),
        P("kvh", "ctx", None),
        P("kvh", "ctx"),
        P("kvh", "ctx"),
    )
    out_specs = P(("ctx", "kvh"), None)
    return jax.shard_map(
        per_device, mesh=mesh, in_specs=in_specs, out_specs=out_specs, check_vma=False
    )
```

```python
import math

import jax
import jax.numpy as jnp
from jax import lax
from jax.experimental import pallas as pl
from jax.experimental.pallas import tpu as pltpu
from jax.sharding import PartitionSpec as P

MESH = pl.DeviceIdType.MESH
BLK = 64
HD = 128
QH = 8
NY = 8
NZ = 8
NCTX = NY * NZ
NKV = 8
WIDTH = QH * HD
TOK = 16
SMAX = 32
NEG = -1e30
SCALE2 = math.log2(math.e) / math.sqrt(HD)
LOG2E = math.log2(math.e)
ROUTES = ((-1, 2, 2, (0, 1)), (1, 4, 2, (0, 1)), (-2, 6, 1, (0,)), (2, 7, 1, (1,)))


def wait_for(ref, sem):
    pltpu.make_async_copy(ref, ref, sem).wait()


def kernel(
    q_ref, k_ref, v_ref, vert_hbm, lists_hbm, cnt_hbm, ord_hbm, out_ref,
    vert_ref, lists_ref, cnt_ref, ord_ref,
    kbuf, vbuf, mrow, mall, msm, pickv, picks, qbuf, q2, gath, stag, kv, va, vb, vsrc, vc,
    acc, mx, ls, bias, ostage, orecv, lstage, lrecv,
    lsem, ssem, s_meta, s_q, s_va, s_vb, s_vc, s_y, s_z, s_out, s_stat,
    r_meta, r_q, r_va, r_vb, r_vc, r_y, r_z, r_out, r_stat,
):
    me = lax.axis_index("ctx")
    h = lax.axis_index("kvh")
    y, z = me // NZ, me % NZ

    def at(yy, zz):
        return lax.rem(yy + 2 * NY, NY) * NZ + lax.rem(zz + 2 * NZ, NZ)

    def push(src, dst, ssem, rsem, ctx, kvh):
        pltpu.make_async_remote_copy(
            src_ref=src, dst_ref=dst, send_sem=ssem, recv_sem=rsem,
            device_id=(ctx, kvh), device_id_type=MESH,
        ).start()

    small = [
        pltpu.make_async_copy(src, dst, ssem.at[i])
        for i, (src, dst) in enumerate((
            (vert_hbm, vert_ref), (lists_hbm, lists_ref), (cnt_hbm, cnt_ref), (ord_hbm, ord_ref),
        ))
    ]
    for copy in small:
        copy.start()
    load_k = pltpu.make_async_copy(k_ref, kbuf, lsem.at[0])
    load_v = pltpu.make_async_copy(v_ref, vbuf, lsem.at[1])

    homes = (at(y + 2, z), at(y - 2, z))

    barrier = pltpu.get_barrier_semaphore()
    for t in range(1, NZ):
        pl.semaphore_signal(barrier, inc=1, device_id=(at(y, z + t), h), device_id_type=MESH)
    for t in range(1, NY):
        pl.semaphore_signal(barrier, inc=1, device_id=(at(y + t, z), h), device_id_type=MESH)
    for home in homes:
        for t in range(1, NKV):
            pl.semaphore_signal(
                barrier, inc=1, device_id=(home, lax.rem(h + t, NKV)), device_id_type=MESH
            )

    for copy in small:
        copy.wait()
    load_k.start()
    load_v.start()
    lane = lax.broadcasted_iota(jnp.int32, (1, 128), 1)
    mrow[0] = jnp.full((1, 128), -1, jnp.int32)
    mrow[0, :, 0:SMAX] = lists_ref[0, 0:1, :]
    mrow[0, :, SMAX:2 * SMAX] = lists_ref[0, 1:2, :]
    row = mrow[0]
    limit = jnp.where(lane < SMAX, cnt_ref[0, 0], cnt_ref[0, 1] + SMAX)
    row = jnp.where(lane < limit, row, -1)
    row = jnp.where(lane == 2 * SMAX, ord_ref[0, 0], row)
    row = jnp.where(lane == 2 * SMAX + 1, ord_ref[0, 1], row)
    spot_of_me = z * NY + y
    mall[spot_of_me] = row

    pl.semaphore_wait(barrier, NZ - 1 + NY - 1 + 2 * (NKV - 1))

    for t in range(1, NY):
        push(mall.at[spot_of_me], mall.at[spot_of_me], s_meta.at[0], r_meta.at[0], at(y + t, z), h)

    token_rows = pl.ds(pl.multiple_of(lax.rem(h, 4) * TOK, TOK), TOK)

    def send_queries(where):
        for i in range(NKV):
            t = lax.rem(h + i, NKV)
            push(
                q_ref.at[:, pl.ds(pl.multiple_of(t * WIDTH, WIDTH), WIDTH)],
                qbuf.at[where * 2 + h // 4, token_rows, :],
                s_q.at[where], r_q.at[where], homes[1 - where], t,
            )

    send_queries(0)
    send_queries(1)

    wait_for(mall.at[pl.ds(0, NY - 1)], r_meta.at[0])
    column = pl.ds(pl.multiple_of(z * NY, NY), NY)
    for t in range(1, NZ):
        push(mall.at[column], mall.at[column], s_meta.at[1], r_meta.at[1], at(y, z + t), h)

    load_k.wait()
    load_v.wait()
    mine = jnp.int32(0)
    for i in range(NKV):
        entry = vert_ref[0, i]
        mine = jnp.where(entry // 32 == me, lax.rem(entry, 32), mine)
    va[0, 0] = kbuf[mine]
    va[0, 1] = vbuf[mine]
    for b in range(1, NZ):
        push(va.at[0], va.at[b], s_va, r_va, at(y, z + b), h)

    wait_for(mall.at[pl.ds(0, NCTX - NY)], r_meta.at[1])
    to_msm = [
        pltpu.make_async_copy(mall.at[z * NY + homes[i] // NZ], msm.at[i], lsem.at[3 + i]) for i in range(2)
    ]
    for copy in to_msm:
        copy.start()
    half = NY // 2
    low = jnp.concatenate([mall[i * NY:i * NY + half].reshape(half, 128) for i in range(NZ)])
    high = jnp.concatenate([mall[i * NY + half:(i + 1) * NY].reshape(half, 128) for i in range(NZ)])
    wide = lax.broadcasted_iota(jnp.int32, (NCTX // 2, 128), 1)
    entries = jnp.where(wide < 2 * SMAX, low, pltpu.roll(high, 2 * SMAX, 1))
    own = lax.shift_right_arithmetic(entries, 5) == me
    local = entries & 31
    first = jnp.min(jnp.where(own, local, 99), axis=1, keepdims=True)
    last = jnp.max(jnp.where(own, local, 0), axis=1, keepdims=True)
    first = jnp.where(first == 99, 0, first)
    tall = lax.broadcasted_iota(jnp.int32, (NCTX // 2, 128), 0)
    pickv[0] = jnp.sum(jnp.where(wide == tall, first + 32 * last, 0), axis=0, keepdims=True)
    to_picks = pltpu.make_async_copy(pickv, picks, lsem.at[2])
    to_picks.start()
    to_picks.wait()

    def stage(ref, dz, slot, dy, which):
        pair = lax.rem(z + dz, NZ) * 4 + lax.rem(y + dy + 2 + NY, 4)
        both = picks[0, 0, pair]
        pick = both & 31 if which == 0 else lax.shift_right_logical(both, 5)
        ref[dz, slot, 0] = kbuf[pick]
        ref[dz, slot, 1] = vbuf[pick]

    def send_own(dz):
        for i in range(2):
            stage(stag, dz, i, 0, i)
        if dz != 0:
            push(
                stag.at[dz, pl.ds(0, 2)], kv.at[dz, pl.ds(0, 2)],
                s_z.at[dz], r_z.at[dz], at(y, z + dz), h,
            )

    def send_y(dz):
        for dy, start, count, which in ROUTES:
            for i in range(count):
                stage(gath, dz, start + i - 2, dy, which[i])
            push(
                gath.at[dz, pl.ds(start - 2, count)], stag.at[dz, pl.ds(start, count)],
                s_y.at[dz], r_y.at[dz], at(y + dy, z), h,
            )

    def send_z(dz):
        wait_for(stag.at[dz, pl.ds(2, 6)], r_y.at[dz])
        push(
            stag.at[dz, pl.ds(2, 6)], kv.at[dz, pl.ds(2, 6)],
            s_z.at[dz], r_z.at[dz], at(y, z + dz), h,
        )

    for dz in (1,):
        send_y(dz)
    for dz in (1, 7, 2, 6, 3, 5, 4, 0,):
        send_own(dz)
    for dz in (7, 2, 6, 3, 5,):
        send_y(dz)
    for dz in (1, 7, 2, 6,):
        send_z(dz)

    owner = vert_ref[0, z] // 32
    wait_for(va.at[pl.ds(1, NZ - 1)], r_va)
    vb[0] = va[lax.rem(z - lax.rem(owner, NZ) + NZ, NZ)]
    for a in range(1, NY):
        push(vb.at[0], vb.at[a], s_vb, r_vb, at(y + a, z), h)

    for dz in (4, 0,):
        send_y(dz)

    for copy in to_msm:
        copy.wait()
    slot = lax.broadcasted_iota(jnp.int32, (NZ, 8 * BLK), 1) // BLK
    back = lax.broadcasted_iota(jnp.int32, (NZ, 8 * BLK), 0)
    step = jnp.where(slot < 2, 0, jnp.where(slot < 4, 1, jnp.where(slot < 6, -1, jnp.where(slot == 6, 2, -2))))
    source = ((y + step) & (NY - 1)) * NZ + ((z - back) & (NZ - 1))

    def scan(t, carry):
        lo, hi = carry
        for i in range(2):
            entry = msm[i, 0, t]
            hit = source == lax.shift_right_arithmetic(entry, 5)
            lo = jnp.where(hit, jnp.minimum(lo, entry), lo)
            hi = jnp.where(hit, jnp.maximum(hi, entry), hi)
        return lo, hi

    lo, hi = lax.fori_loop(
        0, 2 * SMAX, scan,
        (jnp.full((NZ, 8 * BLK), 1 << 20, jnp.int32), jnp.full((NZ, 8 * BLK), -3, jnp.int32)),
    )
    second = (slot == 1) | (slot == 3) | (slot == 5) | (slot == 7)
    held = jnp.where(second, jnp.where(hi > lo, hi, -2), lo)

    stay = msm[0, 0, 2 * SMAX] & 1
    came = msm[0, 0, 2 * SMAX + 1] & 1
    source_block = (stay, 2 + came, 3 - came, 1 - stay)
    for r in range(4):
        block = source_block[r]
        side = block // 2
        first_entry = lax.rem(block, 2) * SMAX

        def member(t, need, side=side, first_entry=first_entry):
            return need | (held == msm[side, 0, first_entry + t]).astype(jnp.int32)

        need = lax.fori_loop(0, SMAX, member, jnp.zeros((NZ, 8 * BLK), jnp.int32))
        bias[r] = jnp.where(need > 0, 0.0, NEG)

    for i in range(8):
        acc[i] = jnp.zeros((256, HD), jnp.float32)
        ls[i] = jnp.zeros((256, 128), jnp.float32)
        mx[i] = jnp.full((256, 128), NEG, jnp.float32)

    for dz in (3, 5,):
        send_z(dz)

    upper = y // 4
    wait_for(vb.at[pl.ds(1, NY - 1)], r_vb)
    vsrc[...] = vb[lax.rem(y - owner // NZ + NY, NY)]
    for j, (low_step, high_step) in enumerate(((0, 1), (4, -1), (2, 3), (-2, -3))):
        target = at(y, z - jnp.where(upper == 1, high_step, low_step))
        if j == 0:
            @pl.when(upper == 0)
            def _():
                vc[0] = vsrc[...]

            @pl.when(upper == 1)
            def _(target=target):
                push(vsrc, vc.at[0], s_vc, r_vc, target, h)
        else:
            push(vsrc, vc.at[j], s_vc, r_vc, target, h)

    for where in range(2):
        wait_for(qbuf.at[pl.ds(where * 2, 2)], r_q.at[where])
    for r in range(4):
        for g in range(QH):
            q2[r * 2 + g // 4, pl.ds((g % 4) * BLK, BLK), :] = qbuf[
                source_block[r], :, pl.ds(g * HD, HD)
            ]

    def attend_rows(r, load, size, dz):
        tiles = (2 * r, 2 * r + 1)
        keys, values = load()
        scores = [
            lax.dot_general(
                q2[i], keys, (((1,), (1,)), ((), ())), preferred_element_type=jnp.float32
            )
            for i in tiles
        ]
        if dz is not None:
            extra = bias[r, dz:dz + 1, :]
            scores = [s + extra for s in scores]
        old = [mx[i] for i in tiles]
        new = [jnp.maximum(o, jnp.max(s, axis=1, keepdims=True)) for o, s in zip(old, scores)]
        shrink = [jnp.exp2((o - n) * SCALE2) for o, n in zip(old, new)]
        weights = [
            jnp.exp2(s * SCALE2 - jnp.concatenate([n * SCALE2] * (size // 128), axis=1))
            for s, n in zip(scores, new)
        ]
        for k, i in enumerate(tiles):
            total = weights[k][:, 0:128]
            for j in range(1, size // 128):
                total = total + weights[k][:, j * 128:(j + 1) * 128]
            ls[i] = ls[i] * shrink[k] + total
            acc[i] = acc[i] * shrink[k] + jnp.dot(
                weights[k].astype(jnp.bfloat16), values, preferred_element_type=jnp.float32
            )
            mx[i] = new[k]

    def attend(load, size, dz):
        def body(r, _):
            attend_rows(r, load, size, dz)
            return 0

        lax.fori_loop(0, 4, body, 0)

    def chunk(dz):
        buf = stag if dz == 0 else kv

        def load():
            return buf[dz, :, 0].reshape(8 * BLK, HD), buf[dz, :, 1].reshape(8 * BLK, HD)

        if dz == 0:
            wait_for(stag.at[0, pl.ds(2, 6)], r_y.at[0])
        else:
            wait_for(kv.at[dz], r_z.at[dz])
        return load, 8 * BLK, dz

    attend(*chunk(1))
    for dz in (4,):
        send_z(dz)
    attend(*chunk(7))
    attend(*chunk(2))
    attend(*chunk(6))
    attend(*chunk(0))
    attend(*chunk(3))
    attend(*chunk(5))

    def wait_vertical(sem):
        @pl.when(upper == 0)
        def _():
            wait_for(vc.at[pl.ds(0, 3)], sem)

        @pl.when(upper == 1)
        def _():
            wait_for(vc, sem)

    wait_vertical(r_vc)
    attend(
        lambda: (vc[:, 0].reshape(4 * BLK, HD), vc[:, 1].reshape(4 * BLK, HD)), 4 * BLK, None
    )
    last_chunks = (chunk(4),)

    lanes = lax.broadcasted_iota(jnp.int32, (BLK, 128), 1)
    spot = lax.broadcasted_iota(jnp.int32, (BLK, 128), 0) & (TOK - 1)

    def finish(r):
        stats = jnp.zeros((BLK, 128), jnp.float32)
        for half in range(2):
            i = r * 2 + half
            total = jnp.sum(ls[i], axis=1, keepdims=True)
            mixed = acc[i] / total
            weight = mx[i] * SCALE2 + jnp.log(total) * LOG2E
            for j in range(4):
                g = half * 4 + j
                rows = slice(j * BLK, (j + 1) * BLK)
                ostage[r, :, g * HD:(g + 1) * HD] = mixed[rows].astype(jnp.bfloat16)
                stats = jnp.where(lanes == g * TOK + spot, weight[rows], stats)
        for t in range(4):
            lstage[r, t] = jnp.sum(stats[t * TOK:(t + 1) * TOK], axis=0, keepdims=True)

    for i in range(4):
        r = (i % 2) * 2 + ((i // 2) ^ ((h // 2) & 1))
        home = homes[i % 2]
        for last in last_chunks:
            attend_rows(r, *last)
        finish(r)
        for k in range(4):
            t = lax.rem(h + k, 4)
            token_device = lax.rem(r, 2) * 4 + t
            push(
                ostage.at[r, pl.ds(pl.multiple_of(t * TOK, TOK), TOK), :], orecv.at[i % 2, h],
                s_out, r_out.at[h], home, token_device,
            )
            push(
                lstage.at[r, t], lrecv.at[i % 2, h], s_stat, r_stat.at[h],
                home, token_device,
            )

    for head in range(NKV):
        wait_for(orecv.at[:, head], r_out.at[head])
        wait_for(lrecv.at[:, head], r_stat.at[head])
        share = 1.0 / (1.0 + jnp.exp2(lrecv[1, head] - lrecv[0, head]))
        share = jnp.broadcast_to(share, (TOK, 128))
        for g in range(QH):
            cols = slice(g * HD, (g + 1) * HD)
            part = jnp.sum(
                jnp.where(lanes[:TOK] == g * TOK + spot[:TOK], share, 0.0), axis=1, keepdims=True
            )
            one = orecv[0, head, :, cols].astype(jnp.float32)
            two = orecv[1, head, :, cols].astype(jnp.float32)
            out_ref[:, head * WIDTH + g * HD:head * WIDTH + (g + 1) * HD] = (
                one * part + two * (1.0 - part)
            ).astype(jnp.bfloat16)

    wait_for(mall.at[pl.ds(0, NY - 1)], s_meta.at[0])
    wait_for(mall.at[pl.ds(0, NCTX - NY)], s_meta.at[1])
    for where in range(2):
        wait_for(qbuf.at[pl.ds(where * 2, 2)], s_q.at[where])
    wait_for(va.at[pl.ds(1, NY - 1)], s_va)
    wait_for(vb.at[pl.ds(1, NZ - 1)], s_vb)
    wait_vertical(s_vc)
    for dz in range(NZ):
        wait_for(gath.at[dz], s_y.at[dz])
    for dz in range(1, NZ):
        wait_for(stag.at[dz], s_z.at[dz])
    wait_for(ostage, s_out)
    wait_for(lstage, s_stat)


def per_device(queries, keys, values, vertical, slash_blocks, slash_count, row_order):
    bf16, f32, i32 = jnp.bfloat16, jnp.float32, jnp.int32
    blocks = keys.shape[1] // BLK
    vmem = pltpu.VMEM
    dma = pltpu.SemaphoreType.DMA
    hbm_spec = pl.BlockSpec(memory_space=pltpu.HBM)
    vmem_spec = pl.BlockSpec(memory_space=pltpu.VMEM)
    return pl.pallas_call(
        kernel,
        out_shape=jax.ShapeDtypeStruct(queries.shape, bf16),
        in_specs=[hbm_spec] * 7,
        out_specs=vmem_spec,
        scratch_shapes=[
            pltpu.SMEM((1, 8), i32),
            vmem((1, 2, SMAX), i32),
            pltpu.SMEM((1, 2), i32),
            pltpu.SMEM((1, 2), i32),
            vmem((blocks, BLK, HD), bf16),
            vmem((blocks, BLK, HD), bf16),
            vmem((1, 1, 128), i32),
            vmem((NCTX, 1, 128), i32),
            pltpu.SMEM((2, 1, 128), i32),
            vmem((1, 1, 128), i32),
            pltpu.SMEM((1, 1, 128), i32),
            vmem((4, BLK, WIDTH), bf16),
            vmem((8, 256, HD), bf16),
            vmem((NZ, 6, 2, BLK, HD), bf16),
            vmem((NZ, 8, 2, BLK, HD), bf16),
            vmem((NZ, 8, 2, BLK, HD), bf16),
            vmem((NY, 2, BLK, HD), bf16),
            vmem((NZ, 2, BLK, HD), bf16),
            vmem((2, BLK, HD), bf16),
            vmem((4, 2, BLK, HD), bf16),
            vmem((8, 256, HD), f32),
            vmem((8, 256, 128), f32),
            vmem((8, 256, 128), f32),
            vmem((4, NZ, 8 * BLK), f32),
            vmem((4, BLK, WIDTH), bf16),
            vmem((2, NKV, TOK, WIDTH), bf16),
            vmem((4, 4, 1, 128), f32),
            vmem((2, NKV, 1, 128), f32),
            dma((5,)),
            dma((4,)),
            dma((2,)), dma((2,)), dma, dma, dma, dma((NZ,)), dma((NZ,)), dma, dma,
            dma((2,)), dma((2,)), dma, dma, dma, dma((NZ,)), dma((NZ,)), dma((NKV,)), dma((NKV,)),
        ],
        compiler_params=pltpu.CompilerParams(
            collective_id=0, has_side_effects=True, vmem_limit_bytes=int(53.6 * 1024 * 1024)
        ),
    )(
        queries,
        keys.reshape(blocks, BLK, HD),
        values.reshape(blocks, BLK, HD),
        vertical, slash_blocks, slash_count, row_order,
    )


def solution(mesh):
    in_specs = (
        P(("ctx", "kvh"), None),
        P("kvh", "ctx", None),
        P("kvh", "ctx", None),
        P("kvh", None),
        P("kvh", "ctx", None),
        P("kvh", "ctx"),
        P("kvh", "ctx"),
    )
    out_specs = P(("ctx", "kvh"), None)
    return jax.shard_map(
        per_device, mesh=mesh, in_specs=in_specs, out_specs=out_specs, check_vma=False
    )
```

```python
import math

import jax
import jax.numpy as jnp
from jax import lax
from jax.experimental import pallas as pl
from jax.experimental.pallas import tpu as pltpu
from jax.sharding import PartitionSpec as P

MESH = pl.DeviceIdType.MESH
BLK = 64
HD = 128
QH = 8
NY = 8
NZ = 8
NCTX = NY * NZ
NKV = 8
WIDTH = QH * HD
TOK = 16
SMAX = 32
NEG = -1e30
SCALE2 = math.log2(math.e) / math.sqrt(HD)
LOG2E = math.log2(math.e)
ROUTES = ((-1, 2, 2, (0, 1)), (1, 4, 2, (0, 1)), (-2, 6, 1, (0,)), (2, 7, 1, (1,)))


def wait_for(ref, sem):
    pltpu.make_async_copy(ref, ref, sem).wait()


def kernel(
    q_ref, k_ref, v_ref, vert_hbm, lists_hbm, cnt_hbm, ord_hbm, out_ref,
    vert_ref, lists_ref, cnt_ref, ord_ref,
    kbuf, vbuf, mrow, mall, msm, pickv, picks, qbuf, q2, gath, stag, kv, va, vb, vsrc, vc,
    acc, mx, ls, bias, ostage, orecv, lstage, lrecv,
    lsem, ssem, s_meta, s_q, s_va, s_vb, s_vc, s_y, s_z, s_out, s_stat,
    r_meta, r_q, r_va, r_vb, r_vc, r_y, r_z, r_out, r_stat,
):
    me = lax.axis_index("ctx")
    h = lax.axis_index("kvh")
    y, z = me // NZ, me % NZ

    def at(yy, zz):
        return lax.rem(yy + 2 * NY, NY) * NZ + lax.rem(zz + 2 * NZ, NZ)

    def push(src, dst, ssem, rsem, ctx, kvh):
        pltpu.make_async_remote_copy(
            src_ref=src, dst_ref=dst, send_sem=ssem, recv_sem=rsem,
            device_id=(ctx, kvh), device_id_type=MESH,
        ).start()

    small = [
        pltpu.make_async_copy(src, dst, ssem.at[i])
        for i, (src, dst) in enumerate((
            (vert_hbm, vert_ref), (lists_hbm, lists_ref), (cnt_hbm, cnt_ref), (ord_hbm, ord_ref),
        ))
    ]
    for copy in small:
        copy.start()
    load_k = pltpu.make_async_copy(k_ref, kbuf, lsem.at[0])
    load_v = pltpu.make_async_copy(v_ref, vbuf, lsem.at[1])

    homes = (at(y + 2, z), at(y - 2, z))

    barrier = pltpu.get_barrier_semaphore()
    for t in range(1, NZ):
        pl.semaphore_signal(barrier, inc=1, device_id=(at(y, z + t), h), device_id_type=MESH)
    for t in range(1, NY):
        pl.semaphore_signal(barrier, inc=1, device_id=(at(y + t, z), h), device_id_type=MESH)
    for home in homes:
        for t in range(1, NKV):
            pl.semaphore_signal(
                barrier, inc=1, device_id=(home, lax.rem(h + t, NKV)), device_id_type=MESH
            )

    for copy in small:
        copy.wait()
    load_k.start()
    load_v.start()
    lane = lax.broadcasted_iota(jnp.int32, (1, 128), 1)
    mrow[0] = jnp.full((1, 128), -1, jnp.int32)
    mrow[0, :, 0:SMAX] = lists_ref[0, 0:1, :]
    mrow[0, :, SMAX:2 * SMAX] = lists_ref[0, 1:2, :]
    row = mrow[0]
    limit = jnp.where(lane < SMAX, cnt_ref[0, 0], cnt_ref[0, 1] + SMAX)
    row = jnp.where(lane < limit, row, -1)
    row = jnp.where(lane == 2 * SMAX, ord_ref[0, 0], row)
    row = jnp.where(lane == 2 * SMAX + 1, ord_ref[0, 1], row)
    spot_of_me = z * NY + y
    mall[spot_of_me] = row

    pl.semaphore_wait(barrier, NZ - 1 + NY - 1 + 2 * (NKV - 1))

    for t in range(1, NY):
        push(mall.at[spot_of_me], mall.at[spot_of_me], s_meta.at[0], r_meta.at[0], at(y + t, z), h)

    token_rows = pl.ds(pl.multiple_of(lax.rem(h, 4) * TOK, TOK), TOK)

    def send_queries(where):
        for i in range(NKV):
            t = lax.rem(h + i, NKV)
            push(
                q_ref.at[:, pl.ds(pl.multiple_of(t * WIDTH, WIDTH), WIDTH)],
                qbuf.at[where * 2 + h // 4, token_rows, :],
                s_q.at[where], r_q.at[where], homes[1 - where], t,
            )

    send_queries(0)
    send_queries(1)

    wait_for(mall.at[pl.ds(0, NY - 1)], r_meta.at[0])
    column = pl.ds(pl.multiple_of(z * NY, NY), NY)
    for t in range(1, NZ):
        push(mall.at[column], mall.at[column], s_meta.at[1], r_meta.at[1], at(y, z + t), h)

    load_k.wait()
    load_v.wait()
    mine = jnp.int32(0)
    for i in range(NKV):
        entry = vert_ref[0, i]
        mine = jnp.where(entry // 32 == me, lax.rem(entry, 32), mine)
    va[0, 0] = kbuf[mine]
    va[0, 1] = vbuf[mine]
    for b in range(1, NZ):
        push(va.at[0], va.at[b], s_va, r_va, at(y, z + b), h)

    wait_for(mall.at[pl.ds(0, NCTX - NY)], r_meta.at[1])
    to_msm = [
        pltpu.make_async_copy(mall.at[z * NY + homes[i] // NZ], msm.at[i], lsem.at[3 + i]) for i in range(2)
    ]
    for copy in to_msm:
        copy.start()
    half = NY // 2
    low = jnp.concatenate([mall[i * NY:i * NY + half].reshape(half, 128) for i in range(NZ)])
    high = jnp.concatenate([mall[i * NY + half:(i + 1) * NY].reshape(half, 128) for i in range(NZ)])
    wide = lax.broadcasted_iota(jnp.int32, (NCTX // 2, 128), 1)
    entries = jnp.where(wide < 2 * SMAX, low, pltpu.roll(high, 2 * SMAX, 1))
    own = lax.shift_right_arithmetic(entries, 5) == me
    local = entries & 31
    first = jnp.min(jnp.where(own, local, 99), axis=1, keepdims=True)
    last = jnp.max(jnp.where(own, local, 0), axis=1, keepdims=True)
    first = jnp.where(first == 99, 0, first)
    tall = lax.broadcasted_iota(jnp.int32, (NCTX // 2, 128), 0)
    pickv[0] = jnp.sum(jnp.where(wide == tall, first + 32 * last, 0), axis=0, keepdims=True)
    to_picks = pltpu.make_async_copy(pickv, picks, lsem.at[2])
    to_picks.start()
    to_picks.wait()

    def stage(ref, dz, slot, dy, which):
        pair = lax.rem(z + dz, NZ) * 4 + lax.rem(y + dy + 2 + NY, 4)
        both = picks[0, 0, pair]
        pick = both & 31 if which == 0 else lax.shift_right_logical(both, 5)
        ref[dz, slot, 0] = kbuf[pick]
        ref[dz, slot, 1] = vbuf[pick]

    def send_own(dz):
        for i in range(2):
            stage(stag, dz, i, 0, i)
        if dz != 0:
            push(
                stag.at[dz, pl.ds(0, 2)], kv.at[dz, pl.ds(0, 2)],
                s_z.at[dz], r_z.at[dz], at(y, z + dz), h,
            )

    def send_y(dz):
        for dy, start, count, which in ROUTES:
            for i in range(count):
                stage(gath, dz, start + i - 2, dy, which[i])
            push(
                gath.at[dz, pl.ds(start - 2, count)], stag.at[dz, pl.ds(start, count)],
                s_y.at[dz], r_y.at[dz], at(y + dy, z), h,
            )

    def send_z(dz):
        wait_for(stag.at[dz, pl.ds(2, 6)], r_y.at[dz])
        push(
            stag.at[dz, pl.ds(2, 6)], kv.at[dz, pl.ds(2, 6)],
            s_z.at[dz], r_z.at[dz], at(y, z + dz), h,
        )

    for dz in (1,):
        send_y(dz)
    for dz in (1, 7, 2, 6, 3, 5, 4, 0,):
        send_own(dz)
    for dz in (7, 2, 6, 3, 5,):
        send_y(dz)
    for dz in (1, 7, 2, 6,):
        send_z(dz)

    owner = vert_ref[0, z] // 32
    wait_for(va.at[pl.ds(1, NZ - 1)], r_va)
    vb[0] = va[lax.rem(z - lax.rem(owner, NZ) + NZ, NZ)]
    for a in range(1, NY):
        push(vb.at[0], vb.at[a], s_vb, r_vb, at(y + a, z), h)

    for dz in (4, 0,):
        send_y(dz)

    for copy in to_msm:
        copy.wait()
    slot = lax.broadcasted_iota(jnp.int32, (NZ, 8 * BLK), 1) // BLK
    back = lax.broadcasted_iota(jnp.int32, (NZ, 8 * BLK), 0)
    step = jnp.where(slot < 2, 0, jnp.where(slot < 4, 1, jnp.where(slot < 6, -1, jnp.where(slot == 6, 2, -2))))
    source = ((y + step) & (NY - 1)) * NZ + ((z - back) & (NZ - 1))

    def scan(t, carry):
        lo, hi = carry
        for i in range(2):
            entry = msm[i, 0, t]
            hit = source == lax.shift_right_arithmetic(entry, 5)
            lo = jnp.where(hit, jnp.minimum(lo, entry), lo)
            hi = jnp.where(hit, jnp.maximum(hi, entry), hi)
        return lo, hi

    lo, hi = lax.fori_loop(
        0, 2 * SMAX, scan,
        (jnp.full((NZ, 8 * BLK), 1 << 20, jnp.int32), jnp.full((NZ, 8 * BLK), -3, jnp.int32)),
    )
    second = (slot == 1) | (slot == 3) | (slot == 5) | (slot == 7)
    held = jnp.where(second, jnp.where(hi > lo, hi, -2), lo)

    stay = msm[0, 0, 2 * SMAX] & 1
    came = msm[0, 0, 2 * SMAX + 1] & 1
    source_block = (stay, 2 + came, 3 - came, 1 - stay)
    for r in range(4):
        block = source_block[r]
        side = block // 2
        first_entry = lax.rem(block, 2) * SMAX

        def member(t, need, side=side, first_entry=first_entry):
            return need | (held == msm[side, 0, first_entry + t]).astype(jnp.int32)

        need = lax.fori_loop(0, SMAX, member, jnp.zeros((NZ, 8 * BLK), jnp.int32))
        bias[r] = jnp.where(need > 0, 0.0, NEG)

    for i in range(8):
        acc[i] = jnp.zeros((256, HD), jnp.float32)
        ls[i] = jnp.zeros((256, 128), jnp.float32)
        mx[i] = jnp.full((256, 128), NEG, jnp.float32)

    for dz in (3, 5,):
        send_z(dz)

    upper = y // 4
    wait_for(vb.at[pl.ds(1, NY - 1)], r_vb)
    vsrc[...] = vb[lax.rem(y - owner // NZ + NY, NY)]
    for j, (low_step, high_step) in enumerate(((0, 1), (4, -1), (2, 3), (-2, -3))):
        target = at(y, z - jnp.where(upper == 1, high_step, low_step))
        if j == 0:
            @pl.when(upper == 0)
            def _():
                vc[0] = vsrc[...]

            @pl.when(upper == 1)
            def _(target=target):
                push(vsrc, vc.at[0], s_vc, r_vc, target, h)
        else:
            push(vsrc, vc.at[j], s_vc, r_vc, target, h)

    for where in range(2):
        wait_for(qbuf.at[pl.ds(where * 2, 2)], r_q.at[where])
    for r in range(4):
        for g in range(QH):
            q2[r * 2 + g // 4, pl.ds((g % 4) * BLK, BLK), :] = qbuf[
                source_block[r], :, pl.ds(g * HD, HD)
            ]

    def attend_rows(r, load, size, dz):
        tiles = (2 * r, 2 * r + 1)
        keys, values = load()
        scores = [
            lax.dot_general(
                q2[i], keys, (((1,), (1,)), ((), ())), preferred_element_type=jnp.float32
            )
            for i in tiles
        ]
        if dz is not None:
            extra = bias[r, dz:dz + 1, :]
            scores = [s + extra for s in scores]
        old = [mx[i] for i in tiles]
        new = [jnp.maximum(o, jnp.max(s, axis=1, keepdims=True)) for o, s in zip(old, scores)]
        shrink = [jnp.exp2((o - n) * SCALE2) for o, n in zip(old, new)]
        weights = [
            jnp.exp2(s * SCALE2 - jnp.concatenate([n * SCALE2] * (size // 128), axis=1))
            for s, n in zip(scores, new)
        ]
        for k, i in enumerate(tiles):
            total = weights[k][:, 0:128]
            for j in range(1, size // 128):
                total = total + weights[k][:, j * 128:(j + 1) * 128]
            ls[i] = ls[i] * shrink[k] + total
            acc[i] = acc[i] * shrink[k] + jnp.dot(
                weights[k].astype(jnp.bfloat16), values, preferred_element_type=jnp.float32
            )
            mx[i] = new[k]

    def attend(load, size, dz):
        def body(r, _):
            attend_rows(r, load, size, dz)
            return 0

        lax.fori_loop(0, 4, body, 0)

    def chunk(dz):
        buf = stag if dz == 0 else kv

        def load():
            return buf[dz, :, 0].reshape(8 * BLK, HD), buf[dz, :, 1].reshape(8 * BLK, HD)

        if dz == 0:
            wait_for(stag.at[0, pl.ds(2, 6)], r_y.at[0])
        else:
            wait_for(kv.at[dz], r_z.at[dz])
        return load, 8 * BLK, dz

    attend(*chunk(1))
    for dz in (4,):
        send_z(dz)
    attend(*chunk(7))
    attend(*chunk(2))
    attend(*chunk(6))
    attend(*chunk(0))
    attend(*chunk(3))
    attend(*chunk(5))

    def wait_vertical(sem):
        @pl.when(upper == 0)
        def _():
            wait_for(vc.at[pl.ds(0, 3)], sem)

        @pl.when(upper == 1)
        def _():
            wait_for(vc, sem)

    wait_vertical(r_vc)
    attend(
        lambda: (vc[:, 0].reshape(4 * BLK, HD), vc[:, 1].reshape(4 * BLK, HD)), 4 * BLK, None
    )
    last_chunks = (chunk(4),)

    lanes = lax.broadcasted_iota(jnp.int32, (BLK, 128), 1)
    spot = lax.broadcasted_iota(jnp.int32, (BLK, 128), 0) & (TOK - 1)

    def finish(r):
        stats = jnp.zeros((BLK, 128), jnp.float32)
        for half in range(2):
            i = r * 2 + half
            total = jnp.sum(ls[i], axis=1, keepdims=True)
            mixed = acc[i] / total
            weight = mx[i] * SCALE2 + jnp.log(total) * LOG2E
            for j in range(4):
                g = half * 4 + j
                rows = slice(j * BLK, (j + 1) * BLK)
                ostage[r, :, g * HD:(g + 1) * HD] = mixed[rows].astype(jnp.bfloat16)
                stats = jnp.where(lanes == g * TOK + spot, weight[rows], stats)
        for t in range(4):
            lstage[r, t] = jnp.sum(stats[t * TOK:(t + 1) * TOK], axis=0, keepdims=True)

    for i in range(4):
        r = (i % 2) * 2 + ((i // 2) ^ ((h // 2) & 1))
        home = homes[i % 2]
        for last in last_chunks:
            attend_rows(r, *last)
        finish(r)
        for k in range(4):
            t = lax.rem(h + k, 4)
            token_device = lax.rem(r, 2) * 4 + t
            push(
                lstage.at[r, t], lrecv.at[i % 2, h], s_stat, r_stat.at[h],
                home, token_device,
            )
        for k in range(4):
            t = lax.rem(h + k, 4)
            token_device = lax.rem(r, 2) * 4 + t
            push(
                ostage.at[r, pl.ds(pl.multiple_of(t * TOK, TOK), TOK), :], orecv.at[i % 2, h],
                s_out, r_out.at[h], home, token_device,
            )

    def merge(i, _):
        head = lax.rem(h + i, NKV)
        wait_for(orecv.at[:, head], r_out.at[head])
        wait_for(lrecv.at[:, head], r_stat.at[head])
        share = 1.0 / (1.0 + jnp.exp2(lrecv[1, head] - lrecv[0, head]))
        share = jnp.broadcast_to(share, (TOK, 128))
        for g in range(QH):
            cols = slice(g * HD, (g + 1) * HD)
            part = jnp.sum(
                jnp.where(lanes[:TOK] == g * TOK + spot[:TOK], share, 0.0), axis=1, keepdims=True
            )
            one = orecv[0, head, :, cols].astype(jnp.float32)
            two = orecv[1, head, :, cols].astype(jnp.float32)
            spread = pl.ds(pl.multiple_of(head * WIDTH + g * HD, HD), HD)
            out_ref[:, spread] = (
                one * part + two * (1.0 - part)
            ).astype(jnp.bfloat16)
        return 0

    lax.fori_loop(0, NKV, merge, 0)

    wait_for(mall.at[pl.ds(0, NY - 1)], s_meta.at[0])
    wait_for(mall.at[pl.ds(0, NCTX - NY)], s_meta.at[1])
    for where in range(2):
        wait_for(qbuf.at[pl.ds(where * 2, 2)], s_q.at[where])
    wait_for(va.at[pl.ds(1, NY - 1)], s_va)
    wait_for(vb.at[pl.ds(1, NZ - 1)], s_vb)
    wait_vertical(s_vc)
    for dz in range(NZ):
        wait_for(gath.at[dz], s_y.at[dz])
    for dz in range(1, NZ):
        wait_for(stag.at[dz], s_z.at[dz])
    wait_for(ostage, s_out)
    wait_for(lstage, s_stat)


def per_device(queries, keys, values, vertical, slash_blocks, slash_count, row_order):
    bf16, f32, i32 = jnp.bfloat16, jnp.float32, jnp.int32
    blocks = keys.shape[1] // BLK
    vmem = pltpu.VMEM
    dma = pltpu.SemaphoreType.DMA
    hbm_spec = pl.BlockSpec(memory_space=pltpu.HBM)
    vmem_spec = pl.BlockSpec(memory_space=pltpu.VMEM)
    return pl.pallas_call(
        kernel,
        out_shape=jax.ShapeDtypeStruct(queries.shape, bf16),
        in_specs=[hbm_spec] * 7,
        out_specs=vmem_spec,
        scratch_shapes=[
            pltpu.SMEM((1, 8), i32),
            vmem((1, 2, SMAX), i32),
            pltpu.SMEM((1, 2), i32),
            pltpu.SMEM((1, 2), i32),
            vmem((blocks, BLK, HD), bf16),
            vmem((blocks, BLK, HD), bf16),
            vmem((1, 1, 128), i32),
            vmem((NCTX, 1, 128), i32),
            pltpu.SMEM((2, 1, 128), i32),
            vmem((1, 1, 128), i32),
            pltpu.SMEM((1, 1, 128), i32),
            vmem((4, BLK, WIDTH), bf16),
            vmem((8, 256, HD), bf16),
            vmem((NZ, 6, 2, BLK, HD), bf16),
            vmem((NZ, 8, 2, BLK, HD), bf16),
            vmem((NZ, 8, 2, BLK, HD), bf16),
            vmem((NY, 2, BLK, HD), bf16),
            vmem((NZ, 2, BLK, HD), bf16),
            vmem((2, BLK, HD), bf16),
            vmem((4, 2, BLK, HD), bf16),
            vmem((8, 256, HD), f32),
            vmem((8, 256, 128), f32),
            vmem((8, 256, 128), f32),
            vmem((4, NZ, 8 * BLK), f32),
            vmem((4, BLK, WIDTH), bf16),
            vmem((2, NKV, TOK, WIDTH), bf16),
            vmem((4, 4, 1, 128), f32),
            vmem((2, NKV, 1, 128), f32),
            dma((5,)),
            dma((4,)),
            dma((2,)), dma((2,)), dma, dma, dma, dma((NZ,)), dma((NZ,)), dma, dma,
            dma((2,)), dma((2,)), dma, dma, dma, dma((NZ,)), dma((NZ,)), dma((NKV,)), dma((NKV,)),
        ],
        compiler_params=pltpu.CompilerParams(
            collective_id=0, has_side_effects=True, vmem_limit_bytes=int(53.67 * 1024 * 1024)
        ),
    )(
        queries,
        keys.reshape(blocks, BLK, HD),
        values.reshape(blocks, BLK, HD),
        vertical, slash_blocks, slash_count, row_order,
    )


def solution(mesh):
    in_specs = (
        P(("ctx", "kvh"), None),
        P("kvh", "ctx", None),
        P("kvh", "ctx", None),
        P("kvh", None),
        P("kvh", "ctx", None),
        P("kvh", "ctx"),
        P("kvh", "ctx"),
    )
    out_specs = P(("ctx", "kvh"), None)
    return jax.shard_map(
        per_device, mesh=mesh, in_specs=in_specs, out_specs=out_specs, check_vma=False
    )
```
